512 devices in a mesh: head: 8 (over z_hi, core), blk: 64 (over x, z_lo, y).
Axes of the slice: x: 4, y: 8, z: 8 (z_hi: 4, z_lo: 2; z = z_hi * 2 + z_lo), core: 2. Of those that a mesh axis runs over, the one named last changes fastest.
Arguments:
- fresh_query: bfloat16 [3584, 2048], P(('head', 'blk')), may hold values from -5 to 5
- fresh_entries: bfloat16 [2, 3584, 2048], P(None, ('head', 'blk')), may hold values from -5 to 5
- cached_entries: bfloat16 [2, 8192, 2048], P(None, ('head', 'blk')), may hold values from -5 to 5
- recompute_rows: int32 [512, 7], P(('head', 'blk')), may hold values from 0 to 15, as said below
- valid_counts: int32 [512], P(('head', 'blk')), may hold values from 1 to 7, as said below
- out_weight: bfloat16 [2048, 3072], P('head'), may hold values from -0.125 to 0.125
- out_gate: float32 [3072], replicated, may hold values from 0.5 to 2
Outputs:
- updated: bfloat16 [3584, 3072], P(('head', 'blk'))
The draws below stay inside these ranges and needn't reach their ends.
Inputs may be any that keep to these rules, and one draw needn't show every extreme that they name: `recompute_rows`: within one device the 7 entries name distinct local rows; entries from valid_counts onward are not used. `valid_counts`: some device uses all 7 slots and some only one.
All inputs are finite; a program needn't handle non-finite values.
Results may differ from the reference program's by a relative error of at most 0.018.
Values may be sent and summed in bfloat16 or wider, within the bound.
A program may use at most 64 MiB of HBM per device.

```python
import jax
import jax.numpy as jnp
from jax import lax

D = 3072
HEADS = 16
HD = 128
TOK_DEV = 16
CAP = 7
SEQ = 8192
ROWS = 3584


def draw_fresh_query(key, part):
    key = jax.random.fold_in(key, 1)
    devices = ROWS // CAP
    values = jnp.clip(1.58 * jax.random.normal(key, (devices, CAP, HEADS * HD), jnp.float32), -5.0, 5.0)
    return values.reshape(ROWS, HEADS * HD).astype(jnp.bfloat16)


def draw_fresh_entries(key, part):
    key = jax.random.fold_in(key, 2)
    key_seed, value_seed = jax.random.split(key)
    devices = ROWS // CAP
    key_part = jnp.clip(1.58 * jax.random.normal(key_seed, (devices, CAP, HEADS * HD), jnp.float32), -5.0, 5.0)
    value_part = jnp.clip(jax.random.normal(value_seed, (devices, CAP, HEADS * HD), jnp.float32), -5.0, 5.0)
    stacked = jnp.stack([key_part.reshape(ROWS, HEADS * HD), value_part.reshape(ROWS, HEADS * HD)])
    return stacked.astype(jnp.bfloat16)


def draw_cached_entries(key, part):
    key = jax.random.fold_in(key, 3)
    key_seed, value_seed = jax.random.split(key)
    key_part = jnp.clip(1.58 * jax.random.normal(key_seed, (SEQ, HEADS * HD), jnp.float32), -5.0, 5.0)
    value_part = jnp.clip(jax.random.normal(value_seed, (SEQ, HEADS * HD), jnp.float32), -5.0, 5.0)
    return jnp.stack([key_part, value_part]).astype(jnp.bfloat16)


def draw_recompute_rows(key, part):
    key = jax.random.fold_in(key, 4)
    devices = ROWS // CAP
    device_keys = jax.random.split(key, devices)
    shuffled = jax.vmap(lambda subkey: jax.random.permutation(subkey, TOK_DEV))(device_keys)
    return shuffled[:, :CAP].astype(jnp.int32)


def draw_valid_counts(key, part):
    key = jax.random.fold_in(key, 5)
    devices = ROWS // CAP
    count_key, pick_key = jax.random.split(key)
    counts = jax.random.randint(count_key, (devices,), 1, CAP + 1)
    full_device = jax.random.randint(pick_key, (), 0, devices)
    device_index = jnp.arange(devices)
    counts = jnp.where(device_index == full_device, CAP, counts)
    counts = jnp.where(device_index == (full_device + devices // 2) % devices, 1, counts)
    return counts.astype(jnp.int32)


def steps_of(rng, shape, cuts, low, high):
    gain, own = 1.0, jax.random.fold_in(rng, 6)
    for position, parts in cuts:
        steps = jnp.exp(jax.random.uniform(jax.random.fold_in(own, position), (parts,), jnp.float32, low / len(cuts), high / len(cuts)))
        gain = gain * jnp.repeat(steps, shape[position] // parts).reshape([-1 if axis == position else 1 for axis in range(len(shape))])
    return gain


def noise(rng, shape, deviation, limit, shards=(), kind=jnp.bfloat16):
    drawn = jax.random.normal(rng, shape, jnp.float32) * deviation
    if len(shards) > 0:
        drawn = steps_of(rng, shape, shards, -0.22, 0.18) * drawn
    return jnp.clip(drawn, min=-limit, max=limit).astype(kind)


def setup_inputs(seed: int = 0) -> dict:
    key_of = jax.random.split(jax.random.key(seed), 8)
    fresh_query = draw_fresh_query(jax.random.fold_in(key_of[7], 71), 0)
    fresh_entries = draw_fresh_entries(jax.random.fold_in(key_of[7], 71), 0)
    cached_entries = draw_cached_entries(jax.random.fold_in(key_of[7], 71), 0)
    recompute_rows = draw_recompute_rows(jax.random.fold_in(key_of[7], 71), 0)
    valid_counts = draw_valid_counts(jax.random.fold_in(key_of[7], 71), 0)
    out_weight = noise(key_of[5], (HEADS * HD, D), (HEADS * HD) ** -0.5, 0.125, ((0, 8),))
    out_gate = jnp.clip(jax.random.uniform(key_of[6], (D,), jnp.float32, 0.5, 2.0), 0.5, 2.0)
    return {"fresh_query": fresh_query, "fresh_entries": fresh_entries, "cached_entries": cached_entries, "recompute_rows": recompute_rows, "valid_counts": valid_counts, "out_weight": out_weight, "out_gate": out_gate}


def reference(fresh_query, fresh_entries, cached_entries, recompute_rows, valid_counts, out_weight, out_gate):
    devices = ROWS // CAP
    score_scale = HD ** -0.5
    slot_index = jnp.arange(CAP, dtype=jnp.int32)
    valid_slots = (slot_index[None, :] < valid_counts[:, None]).reshape(-1)
    targets = (jnp.arange(devices, dtype=jnp.int32)[:, None] * TOK_DEV + recompute_rows).reshape(-1)
    targets = jnp.where(valid_slots, targets, SEQ).astype(jnp.int32)
    keys_values = cached_entries.at[:, targets, :].set(fresh_entries, mode="drop")
    query_heads = fresh_query.reshape(ROWS, HEADS, HD).transpose(1, 0, 2)
    key_heads = keys_values[0].reshape(SEQ, HEADS, HD).transpose(1, 0, 2)
    value_heads = keys_values[1].reshape(SEQ, HEADS, HD).transpose(1, 0, 2)

    def one_head(operands):
        query_part, key_part, value_part = operands
        scores = jnp.dot(query_part, key_part.T, preferred_element_type=jnp.float32) * score_scale
        row_top = jnp.max(scores, axis=1, keepdims=True)
        weights_raw = jnp.exp(scores - row_top)
        denominator = jnp.sum(weights_raw, axis=1, keepdims=True)
        mixture = jnp.dot(weights_raw.astype(jnp.bfloat16), value_part, preferred_element_type=jnp.float32)
        return mixture / denominator

    attention = lax.map(one_head, (query_heads, key_heads, value_heads))
    attention = attention.transpose(1, 0, 2).reshape(ROWS, HEADS * HD).astype(jnp.bfloat16)
    projected = jnp.dot(attention, out_weight, preferred_element_type=jnp.float32) * out_gate[None, :]
    return jnp.where(valid_slots[:, None], projected, 0.0).astype(jnp.bfloat16)
```

```python
import functools
import math

import jax
import jax.numpy as jnp
from jax import lax
from jax.experimental import pallas as pl
from jax.experimental.pallas import tpu as pltpu
from jax.sharding import PartitionSpec as P

HD = 128
HEADS = 16
TOK = 16
CAP = 7
D = 3072
NX, NY, NZ = 4, 8, 4
CHUNKS = 3
HALF = D // 2
CW = HALF // CHUNKS
SCALE2 = (HD ** -0.5) * math.log2(math.e)
MESH = pl.DeviceIdType.MESH
F32, BF16 = jnp.float32, jnp.bfloat16


def kernel(
    q_hbm, fresh_hbm, cached_hbm, rows_ref, cnt_ref, w_hbm, out_ref,
    q_in, fresh_in, cached_in, fresh32, q_out, kv_out, q_land, kv_all, q_all, vt,
    o_out, o_in, st_out, st_in, att, a_in, w_all, p_out, p_in,
    sem_in, qz_s, qz_r, kz_s, kz_r, w_s, w_r, qy_s, qy_r, kx_s, kx_r,
    o_s, o_r, t_s, t_r, a_s, a_r, p_s, p_r,
):
    head = lax.axis_index("head")
    blk = lax.axis_index("blk")
    core = head % 2
    zh = head // 2
    y = blk % NY
    zl = (blk // NY) % 2
    x = blk // (2 * NY)
    me = head * 2 + zl

    def at_z(h):
        return (h // 2, (x * 2 + h % 2) * NY + y)

    def at_x(xx):
        return (head, (xx * 2 + zl) * NY + y)

    def at_y(yy):
        return (head, (x * 2 + zl) * NY + yy)

    def send(src, dst, s_sem, r_sem, dev):
        return pltpu.make_async_remote_copy(
            src_ref=src, dst_ref=dst, send_sem=s_sem, recv_sem=r_sem,
            device_id=dev, device_id_type=MESH,
        )

    right, left = at_x((x + 1) % NX), at_x((x + NX - 1) % NX)

    loads = [
        pltpu.make_async_copy(q_hbm, q_in, sem_in.at[0]),
        pltpu.make_async_copy(fresh_hbm, fresh_in, sem_in.at[1]),
        pltpu.make_async_copy(cached_hbm, cached_in, sem_in.at[2]),
        pltpu.make_async_copy(w_hbm, w_all.at[core], sem_in.at[3]),
    ]
    for load in loads:
        load.start()

    barrier = pltpu.get_barrier_semaphore()

    def greet(t, _):
        pl.semaphore_signal(barrier, inc=1, device_id=at_z((me + t) % HEADS), device_id_type=MESH)
        return 0

    lax.fori_loop(1, HEADS, greet, 0)
    for s in range(1, NY):
        pl.semaphore_signal(barrier, inc=1, device_id=at_y((y + s) % NY), device_id_type=MESH)
    for dev in (right, left):
        pl.semaphore_signal(barrier, inc=1, device_id=dev, device_id_type=MESH)

    loads[0].wait()
    fresh32[0, ...] = jnp.zeros((8, HEADS * HD), F32)
    fresh32[0, 0:CAP, :] = q_in[...].astype(F32)
    for h in range(HEADS):
        rows8 = fresh32[0, :, h * HD:(h + 1) * HD]
        q_out[h] = jnp.concatenate([rows8, jnp.zeros((8, HD), F32)], axis=0).astype(BF16)
    loads[1].wait()
    loads[2].wait()
    for i in range(2):
        fresh32[1 + i, 0:CAP, :] = fresh_in[i].astype(F32)
    count = cnt_ref[0]
    token = lax.broadcasted_iota(jnp.int32, (TOK, HD), 0)
    hits = []
    for c in range(CAP):
        used = jnp.full((TOK, HD), c, jnp.int32) < count
        hits.append((token == rows_ref[0, c]) & used)
    for h in range(HEADS):
        for i in range(2):
            cols = slice(h * HD, (h + 1) * HD)
            merged = cached_in[i, :, cols].astype(F32)
            for c in range(CAP):
                merged = jnp.where(hits[c], fresh32[1 + i, c:c + 1, cols], merged)
            kv_out[h, i * TOK:(i + 1) * TOK, :] = merged.astype(BF16)

    pl.semaphore_wait(barrier, HEADS - 1 + NY - 1 + 2)

    place = (me % 4) * 4 + me // 4
    q_land[place] = q_out[me]
    kv_all[0, 0] = kv_out[me]

    def send_q(t, _):
        h = (me + t) % HEADS
        send(q_out.at[h], q_land.at[place], qz_s.at[t], qz_r.at[t], at_z(h)).start()
        return 0

    def send_kv(t, _):
        h = (me + t) % HEADS
        send(kv_out.at[h], kv_all.at[0, t], kz_s.at[t], kz_r.at[t], at_z(h)).start()
        return 0

    lax.fori_loop(1, HEADS, send_q, 0)
    lax.fori_loop(1, HEADS, send_kv, 0)

    other = (head + 1 - 2 * core, blk)
    w_copy = send(w_hbm, w_all.at[core], w_s, w_r, other)
    w_copy.start()

    def wait_q(t, _):
        h = (me + HEADS - t) % HEADS
        src = (h % 4) * 4 + h // 4
        send(q_out.at[0], q_land.at[src], qz_s.at[t], qz_r.at[t], at_z(h)).wait_recv()
        return 0

    lax.fori_loop(1, HEADS, wait_q, 0)
    q_all[0] = q_land[...].astype(F32)[:, 0:8, :].reshape(HEADS * 8, HD).astype(BF16)
    order = (4, 3, 5, 2, 6, 1, 7)
    for s in order:
        send(q_all.at[0], q_all.at[s], qy_s.at[s], qy_r.at[s], at_y((y + s) % NY)).start()

    lower, upper = pl.ds(0, 8), pl.ds(8, 8)

    def wait_kv(t, _):
        send(kv_out.at[0], kv_all.at[0, t], kz_s.at[t], kz_r.at[t], left).wait_recv()
        return 0

    def kx(i, src, dst, dev):
        return send(kv_all.at[src[0], src[1]], kv_all.at[dst, src[1]], kx_s.at[i], kx_r.at[i], dev)

    copies = [
        kx(0, (0, lower), 1, right),
        kx(1, (0, upper), 2, left),
        kx(2, (0, upper), 1, right),
        kx(3, (0, lower), 2, left),
        kx(4, (1, lower), 3, right),
        kx(5, (2, upper), 3, left),
    ]
    lax.fori_loop(1, 8, wait_kv, 0)
    copies[0].start()
    copies[3].start()
    lax.fori_loop(8, HEADS, wait_kv, 0)
    copies[1].start()
    copies[2].start()
    copies[0].wait_recv()
    copies[4].start()
    copies[1].wait_recv()
    copies[5].start()
    for i in (2, 3, 4, 5):
        copies[i].wait_recv()

    tokens = NX * HEADS * TOK
    keys = kv_all[:, :, 0:TOK, :].reshape(tokens, HD)
    values = kv_all[:, :, TOK:2 * TOK, :].reshape(tokens, HD)
    vt[0:HD, :] = values.astype(F32).T.astype(BF16)
    vt[HD:HD + 16, :] = jnp.ones((16, tokens), BF16)
    for pair in ((4, 3), (5, 2), (6, 1), (7, 0)):
        for s in pair:
            if s:
                send(q_all.at[0], q_all.at[s], qy_s.at[s], qy_r.at[s], left).wait_recv()
        queries = jnp.concatenate([q_all[pair[0]], q_all[pair[1]]], axis=0)
        scores = lax.dot_general(keys, queries, (((1,), (1,)), ((), ())), preferred_element_type=F32)
        top = jnp.max(scores, axis=0, keepdims=True) * SCALE2
        weights = jnp.exp2(scores * SCALE2 - top).astype(BF16)
        mixed = jnp.dot(vt[...], weights, preferred_element_type=F32)
        total = mixed[HD:HD + 1, :]
        mixed = (mixed[0:HD, :] * (1.0 / total)).astype(BF16)
        level = top + jnp.log2(total)
        for n, s in enumerate(pair):
            cols = slice(n * HD, (n + 1) * HD)
            if s == 0:
                o_in[0] = mixed[:, cols]
                st_in[0] = level[:, cols]
            else:
                dev = at_y((y + NY - s) % NY)
                o_out[s] = mixed[:, cols]
                st_out[s] = level[:, cols]
                send(st_out.at[s], st_in.at[s], t_s.at[s], t_r.at[s], dev).start()
                send(o_out.at[s], o_in.at[s], o_s.at[s], o_r.at[s], dev).start()

    for s in range(1, NY):
        send(st_out.at[s], st_in.at[s], t_s.at[s], t_r.at[s], left).wait_recv()
        send(o_out.at[s], o_in.at[s], o_s.at[s], o_r.at[s], left).wait_recv()
    peak = st_in[0]
    for s in range(1, NY):
        peak = jnp.maximum(peak, st_in[s])
    parts = [jnp.exp2(st_in[s] - peak) for s in range(NY)]
    share = 1.0 / functools.reduce(jnp.add, parts)
    mean = functools.reduce(jnp.add, [o_in[s].astype(F32) * (parts[s] * share) for s in range(NY)])
    att[...] = mean.T.astype(BF16)

    def rows_of(quarter):
        return pl.ds(pl.multiple_of(quarter * 32, 32), 32)

    mine = me % 4
    for t in range(1, 4):
        k = (mine + t) % 4
        send(att.at[rows_of(k)], a_in.at[mine], a_s.at[t], a_r.at[t], at_z(zh * 4 + k)).start()
    a_in[mine] = att[rows_of(mine), :]
    loads[3].wait()
    w_wait = send(w_hbm, w_all.at[1 - core], w_s, w_r, other)
    w_wait.wait_recv()
    for t in range(1, 4):
        k = (mine + 4 - t) % 4
        send(att.at[rows_of(0)], a_in.at[k], a_s.at[t], a_r.at[t], left).wait_recv()

    rows = jnp.concatenate([a_in[k] for k in range(4)], axis=1)
    for ci in range(CHUNKS):
        lo, hi = ci * CW, HALF + ci * CW
        sides = []
        for start in (lo, hi):
            w = jnp.concatenate([w_all[0, :, start:start + CW], w_all[1, :, start:start + CW]], axis=0)
            sides.append(jnp.dot(rows, w, preferred_element_type=F32))
        for k in range(NZ):
            block = jnp.concatenate([side[k * 8:(k + 1) * 8] for side in sides], axis=0)
            p_out[ci, k] = block.astype(BF16)
        for t in range(1, NZ):
            k = (zh + t) % NZ
            send(
                p_out.at[ci, k], p_in.at[ci, t], p_s.at[ci, t], p_r.at[ci, t], at_z(k * 4 + mine)
            ).start()
    for ci in range(CHUNKS):
        total = p_out[ci, zh].astype(F32)
        for t in range(1, NZ):
            send(p_out.at[ci, 0], p_in.at[ci, t], p_s.at[ci, t], p_r.at[ci, t], left).wait_recv()
            total = total + p_in[ci, t].astype(F32)
        out_ref[:, ci * CW:(ci + 1) * CW] = total[0:8]
        out_ref[:, HALF + ci * CW:HALF + (ci + 1) * CW] = total[8:16]

    def sent_z(t, _):
        send(q_out.at[0], q_land.at[0], qz_s.at[t], qz_r.at[t], left).wait_send()
        send(kv_out.at[0], kv_all.at[0, 0], kz_s.at[t], kz_r.at[t], left).wait_send()
        return 0

    lax.fori_loop(1, HEADS, sent_z, 0)
    w_copy.wait_send()
    for s in range(1, NY):
        send(q_all.at[0], q_all.at[s], qy_s.at[s], qy_r.at[s], left).wait_send()
        send(st_out.at[s], st_in.at[s], t_s.at[s], t_r.at[s], left).wait_send()
        send(o_out.at[s], o_in.at[s], o_s.at[s], o_r.at[s], left).wait_send()
    for copy in copies:
        copy.wait_send()
    for t in range(1, 4):
        send(att.at[rows_of(0)], a_in.at[0], a_s.at[t], a_r.at[t], left).wait_send()
        for ci in range(CHUNKS):
            send(p_out.at[ci, 0], p_in.at[ci, t], p_s.at[ci, t], p_r.at[ci, t], left).wait_send()


def on_device(fresh_query, fresh_entries, cached_entries, recompute_rows, valid_counts, out_weight, out_gate):
    dma = pltpu.SemaphoreType.DMA
    any_space = pl.BlockSpec(memory_space=pl.ANY)
    smem = pl.BlockSpec(memory_space=pltpu.SMEM)
    width = HEADS * HD
    summed = pl.pallas_call(
        kernel,
        out_shape=jax.ShapeDtypeStruct((8, D), F32),
        in_specs=[any_space, any_space, any_space, smem, smem, any_space],
        out_specs=pl.BlockSpec(memory_space=pltpu.VMEM),
        scratch_shapes=[
            pltpu.VMEM((CAP, width), BF16),
            pltpu.VMEM((2, CAP, width), BF16),
            pltpu.VMEM((2, TOK, width), BF16),
            pltpu.VMEM((3, 8, width), F32),
            pltpu.VMEM((HEADS, 16, HD), BF16),
            pltpu.VMEM((HEADS, 2 * TOK, HD), BF16),
            pltpu.VMEM((HEADS, 16, HD), BF16),
            pltpu.VMEM((NX, HEADS, 2 * TOK, HD), BF16),
            pltpu.VMEM((NY, HEADS * 8, HD), BF16),
            pltpu.VMEM((HD + 16, NX * HEADS * TOK), BF16),
            pltpu.VMEM((NY, HD, HD), BF16),
            pltpu.VMEM((NY, HD, HD), BF16),
            pltpu.VMEM((NY, 1, HD), F32),
            pltpu.VMEM((NY, 1, HD), F32),
            pltpu.VMEM((HD, HD), BF16),
            pltpu.VMEM((4, 32, HD), BF16),
            pltpu.VMEM((2, 2 * HD, D), BF16),
            pltpu.VMEM((CHUNKS, NZ, 16, CW), BF16),
            pltpu.VMEM((CHUNKS, NZ, 16, CW), BF16),
            dma((4,)),
            dma((HEADS,)), dma((HEADS,)), dma((HEADS,)), dma((HEADS,)),
            dma, dma,
            dma((NY,)), dma((NY,)),
            dma((6,)), dma((6,)),
            dma((NY,)), dma((NY,)), dma((NY,)), dma((NY,)),
            dma((4,)), dma((4,)),
            dma((CHUNKS, NZ)), dma((CHUNKS, NZ)),
        ],
        compiler_params=pltpu.CompilerParams(
            collective_id=0, has_side_effects=True, vmem_limit_bytes=48 * 1024 * 1024
        ),
    )(fresh_query, fresh_entries, cached_entries, recompute_rows, valid_counts, out_weight)
    valid = jnp.arange(CAP, dtype=jnp.int32) < valid_counts[0]
    return jnp.where(valid[:, None], summed[:CAP] * out_gate[None, :], 0.0).astype(BF16)


def solution(mesh):
    both = ("head", "blk")
    in_specs = (P(both, None), P(None, both, None), P(None, both, None), P(both, None), P(both), P("head", None), P())
    return jax.shard_map(on_device, mesh=mesh, in_specs=in_specs, out_specs=P(both, None), check_vma=False)
```

```python
import functools
import math

import jax
import jax.numpy as jnp
from jax import lax
from jax.experimental import pallas as pl
from jax.experimental.pallas import tpu as pltpu
from jax.sharding import PartitionSpec as P

HD = 128
HEADS = 16
TOK = 16
CAP = 7
D = 3072
NX, NY, NZ = 4, 8, 4
CHUNKS = 3
HALF = D // 2
CW = HALF // CHUNKS
SCALE2 = (HD ** -0.5) * math.log2(math.e)
MESH = pl.DeviceIdType.MESH
F32, BF16 = jnp.float32, jnp.bfloat16


def kernel(
    q_hbm, fresh_hbm, cached_hbm, rows_hbm, cnt_hbm, w_hbm, out_ref,
    q_in, fresh_in, cached_in, rows_in, cnt_in, fresh32, q_out, kv_out, q_land, kv_all, q_all, vt,
    o_out, o_in, st_out, st_in, att, a_in, w_all, p_out, p_in,
    sem_in, qz_s, qz_r, kz_s, kz_r, w_s, w_r, qy_s, qy_r, kx_s, kx_r,
    o_s, o_r, t_s, t_r, a_s, a_r, p_s, p_r,
):
    head = lax.axis_index("head")
    blk = lax.axis_index("blk")
    core = head % 2
    zh = head // 2
    y = blk % NY
    zl = (blk // NY) % 2
    x = blk // (2 * NY)
    me = head * 2 + zl

    def at_z(h):
        return (h // 2, (x * 2 + h % 2) * NY + y)

    def at_x(xx):
        return (head, (xx * 2 + zl) * NY + y)

    def at_y(yy):
        return (head, (x * 2 + zl) * NY + yy)

    def send(src, dst, s_sem, r_sem, dev):
        return pltpu.make_async_remote_copy(
            src_ref=src, dst_ref=dst, send_sem=s_sem, recv_sem=r_sem,
            device_id=dev, device_id_type=MESH,
        )

    right, left = at_x((x + 1) % NX), at_x((x + NX - 1) % NX)

    loads = [
        pltpu.make_async_copy(q_hbm, q_in, sem_in.at[0]),
        pltpu.make_async_copy(fresh_hbm, fresh_in, sem_in.at[1]),
        pltpu.make_async_copy(cached_hbm, cached_in, sem_in.at[2]),
        pltpu.make_async_copy(w_hbm, w_all.at[core], sem_in.at[3]),
        pltpu.make_async_copy(rows_hbm, rows_in, sem_in.at[4]),
        pltpu.make_async_copy(cnt_hbm, cnt_in, sem_in.at[5]),
    ]
    for load in loads:
        load.start()

    barrier = pltpu.get_barrier_semaphore()

    def greet(t, _):
        pl.semaphore_signal(barrier, inc=1, device_id=at_z((me + t) % HEADS), device_id_type=MESH)
        return 0

    lax.fori_loop(1, HEADS, greet, 0)
    for s in range(1, NY):
        pl.semaphore_signal(barrier, inc=1, device_id=at_y((y + s) % NY), device_id_type=MESH)
    for dev in (right, left):
        pl.semaphore_signal(barrier, inc=1, device_id=dev, device_id_type=MESH)

    loads[0].wait()
    fresh32[0, ...] = jnp.zeros((8, HEADS * HD), F32)
    fresh32[0, 0:CAP, :] = q_in[...].astype(F32)
    for h in range(HEADS):
        rows8 = fresh32[0, :, h * HD:(h + 1) * HD]
        q_out[h] = jnp.concatenate([rows8, jnp.zeros((8, HD), F32)], axis=0).astype(BF16)
    for i in (1, 2, 4, 5):
        loads[i].wait()
    for i in range(2):
        fresh32[1 + i, 0:CAP, :] = fresh_in[:, i, :].astype(F32)
    count = cnt_in[0]
    token = lax.broadcasted_iota(jnp.int32, (TOK, HD), 0)
    hits = []
    for c in range(CAP):
        used = jnp.full((TOK, HD), c, jnp.int32) < count
        hits.append((token == rows_in[0, c]) & used)
    for h in range(HEADS):
        for i in range(2):
            cols = slice(h * HD, (h + 1) * HD)
            merged = cached_in[i, :, cols].astype(F32)
            for c in range(CAP):
                merged = jnp.where(hits[c], fresh32[1 + i, c:c + 1, cols], merged)
            kv_out[h, i * TOK:(i + 1) * TOK, :] = merged.astype(BF16)

    pl.semaphore_wait(barrier, HEADS - 1 + NY - 1 + 2)

    place = (me % 4) * 4 + me // 4
    q_land[place] = q_out[me]
    kv_all[0, 0] = kv_out[me]

    def send_q(t, _):
        h = (me + t) % HEADS
        send(q_out.at[h], q_land.at[place], qz_s.at[t], qz_r.at[t], at_z(h)).start()
        return 0

    def send_kv(t, _):
        h = (me + t) % HEADS
        send(kv_out.at[h], kv_all.at[0, t], kz_s.at[t], kz_r.at[t], at_z(h)).start()
        return 0

    lax.fori_loop(1, HEADS, send_q, 0)
    lax.fori_loop(1, HEADS, send_kv, 0)

    other = (head + 1 - 2 * core, blk)
    w_copy = send(w_hbm, w_all.at[core], w_s, w_r, other)
    w_copy.start()

    def wait_q(t, _):
        h = (me + HEADS - t) % HEADS
        src = (h % 4) * 4 + h // 4
        send(q_out.at[0], q_land.at[src], qz_s.at[t], qz_r.at[t], at_z(h)).wait_recv()
        return 0

    lax.fori_loop(1, HEADS, wait_q, 0)
    q_all[0] = q_land[...].astype(F32)[:, 0:8, :].reshape(HEADS * 8, HD).astype(BF16)
    order = (4, 3, 5, 2, 6, 1, 7)
    for s in order:
        send(q_all.at[0], q_all.at[s], qy_s.at[s], qy_r.at[s], at_y((y + s) % NY)).start()

    lower, upper = pl.ds(0, 8), pl.ds(8, 8)

    def wait_kv(t, _):
        send(kv_out.at[0], kv_all.at[0, t], kz_s.at[t], kz_r.at[t], left).wait_recv()
        return 0

    def kx(i, src, dst, dev):
        return send(kv_all.at[src[0], src[1]], kv_all.at[dst, src[1]], kx_s.at[i], kx_r.at[i], dev)

    copies = [
        kx(0, (0, lower), 1, right),
        kx(1, (0, upper), 2, left),
        kx(2, (0, upper), 1, right),
        kx(3, (0, lower), 2, left),
        kx(4, (1, lower), 3, right),
        kx(5, (2, upper), 3, left),
    ]
    lax.fori_loop(1, 8, wait_kv, 0)
    copies[0].start()
    copies[3].start()
    lax.fori_loop(8, HEADS, wait_kv, 0)
    copies[1].start()
    copies[2].start()
    copies[0].wait_recv()
    copies[4].start()
    copies[1].wait_recv()
    copies[5].start()
    for i in (2, 3, 4, 5):
        copies[i].wait_recv()

    tokens = NX * HEADS * TOK
    keys = kv_all[:, :, 0:TOK, :].reshape(tokens, HD)
    values = kv_all[:, :, TOK:2 * TOK, :].reshape(tokens, HD)
    vt[0:HD, :] = values.astype(F32).T.astype(BF16)
    vt[HD:HD + 16, :] = jnp.ones((16, tokens), BF16)
    for pair in ((4, 3), (5, 2), (6, 1), (7, 0)):
        for s in pair:
            if s:
                send(q_all.at[0], q_all.at[s], qy_s.at[s], qy_r.at[s], left).wait_recv()
        queries = jnp.concatenate([q_all[pair[0]], q_all[pair[1]]], axis=0)
        scores = lax.dot_general(keys, queries, (((1,), (1,)), ((), ())), preferred_element_type=F32)
        top = jnp.max(scores, axis=0, keepdims=True) * SCALE2
        weights = jnp.exp2(scores * SCALE2 - top).astype(BF16)
        mixed = jnp.dot(vt[...], weights, preferred_element_type=F32)
        total = mixed[HD:HD + 1, :]
        mixed = (mixed[0:HD, :] * (1.0 / total)).astype(BF16)
        level = top + jnp.log2(total)
        for n, s in enumerate(pair):
            cols = slice(n * HD, (n + 1) * HD)
            if s == 0:
                o_in[0] = mixed[:, cols]
                st_in[0] = level[:, cols]
            else:
                dev = at_y((y + NY - s) % NY)
                o_out[s] = mixed[:, cols]
                st_out[s] = level[:, cols]
                send(st_out.at[s], st_in.at[s], t_s.at[s], t_r.at[s], dev).start()
                send(o_out.at[s], o_in.at[s], o_s.at[s], o_r.at[s], dev).start()

    for s in range(1, NY):
        send(st_out.at[s], st_in.at[s], t_s.at[s], t_r.at[s], left).wait_recv()
        send(o_out.at[s], o_in.at[s], o_s.at[s], o_r.at[s], left).wait_recv()
    peak = st_in[0]
    for s in range(1, NY):
        peak = jnp.maximum(peak, st_in[s])
    parts = [jnp.exp2(st_in[s] - peak) for s in range(NY)]
    share = 1.0 / functools.reduce(jnp.add, parts)
    mean = functools.reduce(jnp.add, [o_in[s].astype(F32) * (parts[s] * share) for s in range(NY)])
    att[...] = mean.T.astype(BF16)

    def rows_of(quarter):
        return pl.ds(pl.multiple_of(quarter * 32, 32), 32)

    mine = me % 4
    for t in range(1, 4):
        k = (mine + t) % 4
        send(att.at[rows_of(k)], a_in.at[mine], a_s.at[t], a_r.at[t], at_z(zh * 4 + k)).start()
    a_in[mine] = att[rows_of(mine), :]
    loads[3].wait()
    w_wait = send(w_hbm, w_all.at[1 - core], w_s, w_r, other)
    w_wait.wait_recv()
    for t in range(1, 4):
        k = (mine + 4 - t) % 4
        send(att.at[rows_of(0)], a_in.at[k], a_s.at[t], a_r.at[t], left).wait_recv()

    rows = jnp.concatenate([a_in[k] for k in range(4)], axis=1)
    for ci in range(CHUNKS):
        lo, hi = ci * CW, HALF + ci * CW
        sides = []
        for start in (lo, hi):
            w = jnp.concatenate([w_all[0, :, start:start + CW], w_all[1, :, start:start + CW]], axis=0)
            sides.append(jnp.dot(rows, w, preferred_element_type=F32))
        for k in range(NZ):
            block = jnp.concatenate([side[k * 8:(k + 1) * 8] for side in sides], axis=0)
            p_out[ci, k] = block.astype(BF16)
        for t in range(1, NZ):
            k = (zh + t) % NZ
            send(
                p_out.at[ci, k], p_in.at[ci, t], p_s.at[ci, t], p_r.at[ci, t], at_z(k * 4 + mine)
            ).start()
    for ci in range(CHUNKS):
        total = p_out[ci, zh].astype(F32)
        for t in range(1, NZ):
            send(p_out.at[ci, 0], p_in.at[ci, t], p_s.at[ci, t], p_r.at[ci, t], left).wait_recv()
            total = total + p_in[ci, t].astype(F32)
        out_ref[:, ci * CW:(ci + 1) * CW] = total[0:8]
        out_ref[:, HALF + ci * CW:HALF + (ci + 1) * CW] = total[8:16]

    def sent_z(t, _):
        send(q_out.at[0], q_land.at[0], qz_s.at[t], qz_r.at[t], left).wait_send()
        send(kv_out.at[0], kv_all.at[0, 0], kz_s.at[t], kz_r.at[t], left).wait_send()
        return 0

    lax.fori_loop(1, HEADS, sent_z, 0)
    w_copy.wait_send()
    for s in range(1, NY):
        send(q_all.at[0], q_all.at[s], qy_s.at[s], qy_r.at[s], left).wait_send()
        send(st_out.at[s], st_in.at[s], t_s.at[s], t_r.at[s], left).wait_send()
        send(o_out.at[s], o_in.at[s], o_s.at[s], o_r.at[s], left).wait_send()
    for copy in copies:
        copy.wait_send()
    for t in range(1, 4):
        send(att.at[rows_of(0)], a_in.at[0], a_s.at[t], a_r.at[t], left).wait_send()
        for ci in range(CHUNKS):
            send(p_out.at[ci, 0], p_in.at[ci, t], p_s.at[ci, t], p_r.at[ci, t], left).wait_send()


def on_device(fresh_query, fresh_entries, cached_entries, recompute_rows, valid_counts, out_weight, out_gate):
    dma = pltpu.SemaphoreType.DMA
    any_space = pl.BlockSpec(memory_space=pl.ANY)
    width = HEADS * HD
    summed = pl.pallas_call(
        kernel,
        out_shape=jax.ShapeDtypeStruct((8, D), F32),
        in_specs=[any_space] * 6,
        out_specs=pl.BlockSpec(memory_space=pltpu.VMEM),
        scratch_shapes=[
            pltpu.VMEM((CAP, width), BF16),
            pltpu.VMEM((CAP, 2, width), BF16),
            pltpu.VMEM((2, TOK, width), BF16),
            pltpu.SMEM((1, CAP), jnp.int32),
            pltpu.SMEM((1,), jnp.int32),
            pltpu.VMEM((3, 8, width), F32),
            pltpu.VMEM((HEADS, 16, HD), BF16),
            pltpu.VMEM((HEADS, 2 * TOK, HD), BF16),
            pltpu.VMEM((HEADS, 16, HD), BF16),
            pltpu.VMEM((NX, HEADS, 2 * TOK, HD), BF16),
            pltpu.VMEM((NY, HEADS * 8, HD), BF16),
            pltpu.VMEM((HD + 16, NX * HEADS * TOK), BF16),
            pltpu.VMEM((NY, HD, HD), BF16),
            pltpu.VMEM((NY, HD, HD), BF16),
            pltpu.VMEM((NY, 1, HD), F32),
            pltpu.VMEM((NY, 1, HD), F32),
            pltpu.VMEM((HD, HD), BF16),
            pltpu.VMEM((4, 32, HD), BF16),
            pltpu.VMEM((2, 2 * HD, D), BF16),
            pltpu.VMEM((CHUNKS, NZ, 16, CW), BF16),
            pltpu.VMEM((CHUNKS, NZ, 16, CW), BF16),
            dma((6,)),
            dma((HEADS,)), dma((HEADS,)), dma((HEADS,)), dma((HEADS,)),
            dma, dma,
            dma((NY,)), dma((NY,)),
            dma((6,)), dma((6,)),
            dma((NY,)), dma((NY,)), dma((NY,)), dma((NY,)),
            dma((4,)), dma((4,)),
            dma((CHUNKS, NZ)), dma((CHUNKS, NZ)),
        ],
        compiler_params=pltpu.CompilerParams(
            collective_id=0, has_side_effects=True, vmem_limit_bytes=60 * 1024 * 1024
        ),
    )(fresh_query, fresh_entries.transpose(1, 0, 2), cached_entries, recompute_rows, valid_counts, out_weight)
    valid = jnp.arange(CAP, dtype=jnp.int32) < valid_counts[0]
    return jnp.where(valid[:, None], summed[:CAP] * out_gate[None, :], 0.0).astype(BF16)


def solution(mesh):
    both = ("head", "blk")
    in_specs = (P(both, None), P(None, both, None), P(None, both, None), P(both, None), P(both), P("head", None), P())
    return jax.shard_map(on_device, mesh=mesh, in_specs=in_specs, out_specs=P(both, None), check_vma=False)
```

```python
import functools
import math

import jax
import jax.numpy as jnp
from jax import lax
from jax.experimental import pallas as pl
from jax.experimental.pallas import tpu as pltpu
from jax.sharding import PartitionSpec as P

HD = 128
HEADS = 16
TOK = 16
CAP = 7
D = 3072
NX, NY, NZ, CHIPS = 4, 8, 4, 8
CHUNKS = 3
HALF = D // 2
CW = HALF // CHUNKS
SCALE2 = (HD ** -0.5) * math.log2(math.e)
MESH = pl.DeviceIdType.MESH
F32, BF16 = jnp.float32, jnp.bfloat16

GROUPS = ((1, 7), (2, 6), (3, 5), (0, 4))
SLOT = {(dz, dc): g * 4 + dc * 2 + e for g, pair in enumerate(GROUPS) for e, dz in enumerate(pair) for dc in range(2)}
SELF = SLOT[0, 0]
NEAR_FIRST = sorted((k for k in SLOT if k != (0, 0)), key=lambda k: min(k[0], CHIPS - k[0]))
FAR_FIRST = NEAR_FIRST[::-1]
PAIRS = ((4, 3), (5, 2), (6, 1), (7, 0))


def kernel(
    q_hbm, fresh_hbm, cached_hbm, rows_hbm, cnt_hbm, w_hbm, out_ref,
    q_in, fresh_in, cached_in, rows_in, cnt_in, fresh32, q_out, kv_out, q_land, kv_all, q_all, vt,
    top_ref, mix_ref, o_out, o_in, st_out, st_in, w_all, p_out, p_in,
    sem_in, qz_s, qz_r, kz_s, kz_r, w_s, w_r, qy_s, qy_r, kx_s, kx_r, o_s, o_r, t_s, t_r, p_s, p_r,
):
    head = lax.axis_index("head")
    blk = lax.axis_index("blk")
    core = head % 2
    zh = head // 2
    y = blk % NY
    zl = (blk // NY) % 2
    x = blk // (2 * NY)
    chip = zh * 2 + zl

    def at_z(dz, dc):
        z, c = (chip + dz) % CHIPS, (core + dc) % 2
        return ((z // 2) * 2 + c, (x * 2 + z % 2) * NY + y)

    def head_of(dz, dc):
        z, c = (chip + dz) % CHIPS, (core + dc) % 2
        return (z // 2) * 4 + c * 2 + z % 2

    def at_x(dx):
        return (head, (((x + dx) % NX) * 2 + zl) * NY + y)

    def at_y(dy):
        return (head, (x * 2 + zl) * NY + (y + dy) % NY)

    def at_o(dy, odd, dc):
        return (zh * 2 + (core + dc) % 2, (x * 2 + (zl + odd) % 2) * NY + (y + dy) % NY)

    def at_p(b):
        return (((zh + b) % NZ) * 2 + core, blk)

    def send(src, dst, s_sem, r_sem, dev):
        return pltpu.make_async_remote_copy(
            src_ref=src, dst_ref=dst, send_sem=s_sem, recv_sem=r_sem,
            device_id=dev, device_id_type=MESH,
        )

    loads = [
        pltpu.make_async_copy(q_hbm, q_in, sem_in.at[0]),
        pltpu.make_async_copy(fresh_hbm, fresh_in, sem_in.at[1]),
        pltpu.make_async_copy(cached_hbm, cached_in, sem_in.at[2]),
        pltpu.make_async_copy(rows_hbm, rows_in, sem_in.at[3]),
        pltpu.make_async_copy(cnt_hbm, cnt_in, sem_in.at[4]),
        pltpu.make_async_copy(w_hbm, w_all.at[0], sem_in.at[5]),
    ]
    for load in loads[:5]:
        load.start()

    barrier = pltpu.get_barrier_semaphore()
    partners = [at_z(dz, dc) for dz, dc in FAR_FIRST]
    partners += [at_y(dy) for dy in (4, 3, 5, 2, 6, 1, 7)] + [at_x(dx) for dx in (2, 1, 3)]
    for dev in partners:
        pl.semaphore_signal(barrier, inc=1, device_id=dev, device_id_type=MESH)

    loads[0].wait()
    fresh32[0, ...] = jnp.zeros((8, HEADS * HD), F32)
    fresh32[0, 0:CAP, :] = q_in[...].astype(F32)

    def lanes(h):
        return pl.ds(pl.multiple_of(h * HD, HD), HD)

    for place in [(0, 0)] + FAR_FIRST:
        rows8 = fresh32[0, :, lanes(head_of(*place))]
        q_out[SLOT[place]] = jnp.concatenate([rows8, jnp.zeros((8, HD), F32)], axis=0).astype(BF16)
    q_land[SELF] = q_out[SELF]
    pl.semaphore_wait(barrier, len(partners))

    def z_copy(out, land, s_sem, r_sem, place):
        back = SLOT[(CHIPS - place[0]) % CHIPS, place[1]]
        return send(out.at[SLOT[place]], land.at[back], s_sem.at[SLOT[place]], r_sem.at[back], at_z(*place))

    for place in FAR_FIRST:
        z_copy(q_out, q_land, qz_s, qz_r, place).start()

    for i in (1, 2, 3, 4):
        loads[i].wait()
    for i in range(2):
        fresh32[1 + i, 0:CAP, :] = fresh_in[:, i, :].astype(F32)
    count = cnt_in[0, 0]
    token = lax.broadcasted_iota(jnp.int32, (TOK, HD), 0)
    hits = []
    for c in range(CAP):
        used = jnp.full((TOK, HD), c, jnp.int32) < count
        hits.append((token == rows_in[0, c]) & used)

    def merged(h, i):
        rows = cached_in[i, :, lanes(h)].astype(F32)
        for c in range(CAP):
            rows = jnp.where(hits[c], fresh32[1 + i, c:c + 1, lanes(h)], rows)
        return rows.astype(BF16)

    for place in NEAR_FIRST:
        for i in range(2):
            kv_out[SLOT[place], i * TOK:(i + 1) * TOK, :] = merged(head_of(*place), i)
        z_copy(kv_out, kv_all.at[0], kz_s, kz_r, place).start()
    for i in range(2):
        kv_all[0, SELF, i * TOK:(i + 1) * TOK, :] = merged(head_of(0, 0), i)

    loads[5].start()
    w_copy = send(w_hbm, w_all.at[1], w_s, w_r, at_z(0, 1))
    w_copy.start()

    def qy(g, s):
        part = pl.ds(g * 32, 32)
        return send(q_all.at[0, part], q_all.at[s, part], qy_s.at[g, s], qy_r.at[g, s], at_y(s))

    def kx(g, s):
        part = pl.ds(g * 4, 4)
        return send(kv_all.at[0, part], kv_all.at[s, part], kx_s.at[g, s], kx_r.at[g, s], at_x(s))

    for g in range(4):
        for n in range(g * 4, g * 4 + 4):
            if n != SELF:
                send(q_out.at[n], q_land.at[n], qz_s.at[n], qz_r.at[n], at_x(1)).wait_recv()
        packed = q_land[g * 4:(g + 1) * 4].astype(F32)[:, 0:8, :].reshape(32, HD)
        q_all[0, g * 32:(g + 1) * 32, :] = packed.astype(BF16)
        for s in (4, 3, 5, 2, 6, 1, 7):
            qy(g, s).start()
    for g in range(4):
        for n in range(g * 4, g * 4 + 4):
            if n != SELF:
                send(kv_out.at[n], kv_all.at[0, n], kz_s.at[n], kz_r.at[n], at_x(1)).wait_recv()
        for s in (2, 1, 3):
            kx(g, s).start()

    tokens = HEADS * TOK
    vt[HD:HD + 16, :] = jnp.ones((16, tokens), BF16)

    def attend(slot, number, first):
        keys = kv_all[slot, :, 0:TOK, :].reshape(tokens, HD)
        queries = jnp.concatenate([q_all[s] for s in PAIRS[number]], axis=0)
        scores = lax.dot_general(keys, queries, (((1,), (1,)), ((), ())), preferred_element_type=F32)
        top = jnp.max(scores, axis=0, keepdims=True) * SCALE2
        if not first:
            old = top_ref[number]
            top = jnp.maximum(top, old)
        weights = jnp.exp2(scores * SCALE2 - top).astype(BF16)
        mixed = jnp.dot(vt[...], weights, preferred_element_type=F32)
        if not first:
            mixed = mixed + mix_ref[number] * jnp.exp2(old - top)
        return top, mixed

    def t_copy(s, g):
        dev = at_o(NY - s, 1 - g // 2, g % 2)
        return send(st_out.at[s], st_in.at[g, s], t_s.at[s, g], t_r.at[s, g], dev)

    def o_copy(s, g):
        dev = at_o(NY - s, 1 - g // 2, g % 2)
        return send(o_out.at[s, :, g], o_in.at[g, :, s], o_s.at[s, g], o_r.at[s, g], dev)

    for step, slot in enumerate((0, 1, 3, 2)):
        if slot:
            for g in range(4):
                kx(g, slot).wait_recv()
        vt[0:HD, :] = kv_all[slot, :, TOK:2 * TOK, :].reshape(tokens, HD).astype(F32).T.astype(BF16)
        for number in (3, 2, 1, 0) if step == 0 else (0, 1, 2, 3):
            if step == 0:
                for s in PAIRS[number]:
                    if s:
                        for g in range(4):
                            qy(g, s).wait_recv()
            top, mixed = attend(slot, number, step == 0)
            if step < NX - 1:
                top_ref[number] = top
                mix_ref[number] = mixed
                continue
            total = mixed[HD:HD + 1, :]
            level = top + jnp.log2(total)
            rows = (mixed[0:HD, :] * (1.0 / total)).T.astype(BF16)
            for n, s in enumerate(PAIRS[number]):
                st_out[s] = level[:, n * HD:(n + 1) * HD]
                o_out[s] = rows[n * HD:(n + 1) * HD].reshape(2, 4, 16, HD)
                for g in range(4):
                    if (s, g) != (0, 2):
                        t_copy(s, g).start()
                        o_copy(s, g).start()
    st_in[2, 0] = st_out[0]
    o_in[2, :, 0] = o_out[0, :, 2]

    remote = [(s, g) for s in (4, 3, 5, 2, 6, 1, 7, 0) for g in range(4) if (s, g) != (0, 2)]
    for s, g in remote:
        t_copy(s, g).wait_recv()
    levels = []
    row8 = lax.broadcasted_iota(jnp.int32, (8, HD), 0)
    lane8 = lax.broadcasted_iota(jnp.int32, (8, HD), 1)
    for g in range(4):
        seen = jnp.concatenate([st_in[g, s] for s in range(NY)], axis=0)
        seen = pltpu.roll(seen, 0, 1, stride=16, stride_axis=0)
        for i in range(2):
            moved = pltpu.roll(seen, (HD - i * 64 - g * 16) % HD, 1)
            levels.append(jnp.sum(jnp.where(lane8 // 16 == row8, moved, 0.0), axis=0, keepdims=True))
    levels = jnp.concatenate(levels, axis=0)
    peak = levels
    for shift in (16, 32, 64):
        peak = jnp.maximum(peak, pltpu.roll(peak, shift, 1))
    parts = jnp.exp2(levels - peak)
    total = parts
    for shift in (16, 32, 64):
        total = total + pltpu.roll(total, shift, 1)
    shares = parts / total

    row = lax.broadcasted_iota(jnp.int32, (32, HD), 0)
    lane = lax.broadcasted_iota(jnp.int32, (32, HD), 1)
    owner = row // 8

    def wanted(order):
        block = jnp.where(owner == 0, order[0], jnp.where(owner == 1, order[1], jnp.where(owner == 2, order[2], order[3])))
        return block * 8 + row % 8

    even = wanted((2, 0, 3, 1))
    odd = jnp.where(zl == 1, wanted((0, 2, 3, 1)), wanted((1, 0, 2, 3)))
    for s, g in remote:
        o_copy(s, g).wait_recv()
    mean = []
    for g in range(4):
        place = odd if g < 2 else even
        mix = [
            jnp.where(place == i * 16 + lane % 16, shares[g * 2 + i:g * 2 + i + 1, :], 0.0) for i in range(2)
        ]
        mix = jnp.concatenate(mix, axis=1).astype(BF16)
        mean.append(jnp.dot(mix, o_in[g].reshape(2 * HD, HD), preferred_element_type=F32))
    heads4 = [jnp.where(zl == z, mean[2 + dc], mean[dc]) for dc in range(2) for z in range(2)]
    rows = jnp.concatenate(heads4, axis=1).astype(BF16)

    loads[5].wait()
    send(w_hbm, w_all.at[1], w_s, w_r, at_z(0, 1)).wait_recv()

    def p_copy(ci, b):
        return send(p_out.at[ci, b], p_in.at[ci, b], p_s.at[ci, b], p_r.at[ci, b], at_p(b))

    for ci in range(CHUNKS):
        sides = []
        for start in (ci * CW, HALF + ci * CW):
            w = jnp.concatenate([w_all[0, :, start:start + CW], w_all[1, :, start:start + CW]], axis=0)
            sides.append(jnp.dot(rows, w, preferred_element_type=F32))
        for b in (2, 1, 3, 0):
            block = jnp.concatenate([side[b * 8:(b + 1) * 8] for side in sides], axis=0)
            p_out[ci, b] = block.astype(BF16)
            if b:
                p_copy(ci, b).start()
    valid = lax.broadcasted_iota(jnp.int32, (8, CW), 0) < count
    for ci in range(CHUNKS):
        total = p_out[ci, 0].astype(F32)
        for b in (1, 3, 2):
            p_copy(ci, b).wait_recv()
            total = total + p_in[ci, b].astype(F32)
        out_ref[:, ci * CW:(ci + 1) * CW] = jnp.where(valid, total[0:8], 0.0)
        out_ref[:, HALF + ci * CW:HALF + (ci + 1) * CW] = jnp.where(valid, total[8:16], 0.0)

    for place in NEAR_FIRST:
        z_copy(q_out, q_land, qz_s, qz_r, place).wait_send()
        z_copy(kv_out, kv_all.at[0], kz_s, kz_r, place).wait_send()
    w_copy.wait_send()
    for g in range(4):
        for s in range(1, NY):
            qy(g, s).wait_send()
        for s in range(1, NX):
            kx(g, s).wait_send()
    for s, g in remote:
        t_copy(s, g).wait_send()
        o_copy(s, g).wait_send()
    for ci in range(CHUNKS):
        for b in range(1, NZ):
            p_copy(ci, b).wait_send()


def on_device(fresh_query, fresh_entries, cached_entries, recompute_rows, valid_counts, out_weight, out_gate):
    dma = pltpu.SemaphoreType.DMA
    width = HEADS * HD
    summed = pl.pallas_call(
        kernel,
        out_shape=jax.ShapeDtypeStruct((8, D), F32),
        in_specs=[pl.BlockSpec(memory_space=pl.ANY)] * 6,
        out_specs=pl.BlockSpec(memory_space=pltpu.VMEM),
        scratch_shapes=[
            pltpu.VMEM((CAP, width), BF16),
            pltpu.VMEM((CAP, 2, width), BF16),
            pltpu.VMEM((2, TOK, width), BF16),
            pltpu.SMEM((1, CAP), jnp.int32),
            pltpu.SMEM((1, 1), jnp.int32),
            pltpu.VMEM((3, 8, width), F32),
            pltpu.VMEM((HEADS, 16, HD), BF16),
            pltpu.VMEM((HEADS, 2 * TOK, HD), BF16),
            pltpu.VMEM((HEADS, 16, HD), BF16),
            pltpu.VMEM((NX, HEADS, 2 * TOK, HD), BF16),
            pltpu.VMEM((NY, HEADS * 8, HD), BF16),
            pltpu.VMEM((HD + 16, HEADS * TOK), BF16),
            pltpu.VMEM((4, 1, 2 * HD), F32),
            pltpu.VMEM((4, HD + 16, 2 * HD), F32),
            pltpu.VMEM((NY, 2, 4, 16, HD), BF16),
            pltpu.VMEM((4, 2, NY, 16, HD), BF16),
            pltpu.VMEM((NY, 1, HD), F32),
            pltpu.VMEM((4, NY, 1, HD), F32),
            pltpu.VMEM((2, 2 * HD, D), BF16),
            pltpu.VMEM((CHUNKS, NZ, 16, CW), BF16),
            pltpu.VMEM((CHUNKS, NZ, 16, CW), BF16),
            dma((6,)),
            dma((HEADS,)), dma((HEADS,)), dma((HEADS,)), dma((HEADS,)),
            dma, dma,
            dma((4, NY)), dma((4, NY)),
            dma((4, NX)), dma((4, NX)),
            dma((NY, 4)), dma((NY, 4)), dma((NY, 4)), dma((NY, 4)),
            dma((CHUNKS, NZ)), dma((CHUNKS, NZ)),
        ],
        compiler_params=pltpu.CompilerParams(
            collective_id=0, has_side_effects=True, vmem_limit_bytes=60 * 1024 * 1024
        ),
    )(fresh_query, fresh_entries.transpose(1, 0, 2), cached_entries, recompute_rows, valid_counts.reshape(1, 1), out_weight)
    return (summed[:CAP] * out_gate[None, :]).astype(BF16)


def solution(mesh):
    both = ("head", "blk")
    in_specs = (P(both, None), P(None, both, None), P(None, both, None), P(both, None), P(both), P("head", None), P())
    return jax.shard_map(on_device, mesh=mesh, in_specs=in_specs, out_specs=P(both, None), check_vma=False)
```

```python
import functools
import math

import jax
import jax.numpy as jnp
from jax import lax
from jax.experimental import pallas as pl
from jax.experimental.pallas import tpu as pltpu
from jax.sharding import PartitionSpec as P

HD = 128
HEADS = 16
TOK = 16
CAP = 7
D = 3072
NX, NY, NZ, CHIPS = 4, 8, 4, 8
CHUNKS = 3
HALF = D // 2
CW = HALF // CHUNKS
SCALE2 = (HD ** -0.5) * math.log2(math.e)
MESH = pl.DeviceIdType.MESH
F32, BF16 = jnp.float32, jnp.bfloat16

PLACES = [(dz, dc) for dz in range(CHIPS) for dc in range(2)]


def slots(groups):
    return {(dz, dc): g * 4 + dc * 2 + e for g, pair in enumerate(groups) for e, dz in enumerate(pair) for dc in range(2)}


KV_SLOT = slots(((1, 7), (2, 6), (3, 5), (0, 4)))
Q_SLOT = slots(((1, 5), (3, 7), (0, 4), (2, 6)))
NEAR_FIRST = sorted((k for k in PLACES if k != (0, 0)), key=lambda k: min(k[0], CHIPS - k[0]))
FAR_FIRST = NEAR_FIRST[::-1]
ORDER = (4, 3, 5, 2, 6, 1, 7, 0)


def kernel(
    q_hbm, fresh_hbm, cached_hbm, rows_hbm, cnt_hbm, w_hbm, out_ref,
    q_in, fresh_in, cached_in, rows_in, cnt_in, fresh32, q_out, kv_out, q_land, kv_all, q_all, vt,
    top_ref, mix_ref, o_out, o_in, st_out, st_in, w_all, p_out, p_in,
    sem_in, qz_s, qz_r, kz_s, kz_r, w_s, w_r, qy_s, qy_r, kx_s, kx_r, o_s, o_r, t_s, t_r, p_s, p_r,
):
    head = lax.axis_index("head")
    blk = lax.axis_index("blk")

    def div(a, b):
        return lax.div(a, jnp.int32(b))

    def rem(a, b):
        return lax.rem(a, jnp.int32(b))

    core, zh = rem(head, 2), div(head, 2)
    y, zl, x = rem(blk, NY), rem(div(blk, NY), 2), div(blk, 2 * NY)
    chip = zh * 2 + zl
    ups = [rem(chip + dz, CHIPS) for dz in range(CHIPS)]
    cores = [core, 1 - core]

    def at_z(dz, dc):
        return (div(ups[dz], 2) * 2 + cores[dc], (x * 2 + rem(ups[dz], 2)) * NY + y)

    def head_of(dz, dc):
        return div(ups[dz], 2) * 4 + cores[dc] * 2 + rem(ups[dz], 2)

    def at_x(dx):
        return (head, (rem(x + dx, NX) * 2 + zl) * NY + y)

    def at_y(dy):
        return (head, (x * 2 + zl) * NY + rem(y + dy, NY))

    def at_o(dy, odd, dc):
        return (zh * 2 + cores[dc], (x * 2 + (1 - zl if odd else zl)) * NY + rem(y + dy, NY))

    def at_p(b):
        return (rem(zh + b, NZ) * 2 + core, blk)

    def send(src, dst, s_sem, r_sem, dev):
        return pltpu.make_async_remote_copy(
            src_ref=src, dst_ref=dst, send_sem=s_sem, recv_sem=r_sem,
            device_id=dev, device_id_type=MESH,
        )

    def arrived(ref, sem):
        send(ref, ref, sem, sem, at_x(1)).wait_recv()

    def left(ref, sem):
        send(ref, ref, sem, sem, at_x(1)).wait_send()

    loads = [
        pltpu.make_async_copy(q_hbm, q_in, sem_in.at[0]),
        pltpu.make_async_copy(fresh_hbm, fresh_in, sem_in.at[1]),
        pltpu.make_async_copy(cached_hbm, cached_in, sem_in.at[2]),
        pltpu.make_async_copy(rows_hbm, rows_in, sem_in.at[3]),
        pltpu.make_async_copy(cnt_hbm, cnt_in, sem_in.at[4]),
        pltpu.make_async_copy(w_hbm, w_all.at[0], sem_in.at[5]),
    ]
    barrier = pltpu.get_barrier_semaphore()
    partners = [at_z(dz, dc) for dz, dc in FAR_FIRST]
    partners += [at_y(dy) for dy in ORDER[:7]] + [at_x(dx) for dx in (2, 1, 3)]
    for dev in partners:
        pl.semaphore_signal(barrier, inc=1, device_id=dev, device_id_type=MESH)
    for load in loads[:5]:
        load.start()

    fresh32[0, ...] = jnp.zeros((8, HEADS * HD), F32)
    loads[0].wait()
    fresh32[0, 0:CAP, :] = q_in[...].astype(F32)

    def lanes(h):
        return pl.ds(pl.multiple_of(h * HD, HD), HD)

    for place in [(0, 0)] + FAR_FIRST:
        rows8 = fresh32[0, :, lanes(head_of(*place))]
        q_out[Q_SLOT[place]] = jnp.concatenate([rows8, jnp.zeros((8, HD), F32)], axis=0).astype(BF16)
    q_land[Q_SLOT[0, 0]] = q_out[Q_SLOT[0, 0]]
    pl.semaphore_wait(barrier, len(partners))

    def z_send(out, land, s_sem, r_sem, table, place):
        back = table[(CHIPS - place[0]) % CHIPS, place[1]]
        send(out.at[table[place]], land.at[back], s_sem, r_sem.at[back // 4], at_z(*place)).start()

    for place in FAR_FIRST:
        z_send(q_out, q_land, qz_s, qz_r, Q_SLOT, place)

    for i in (1, 2, 3, 4):
        loads[i].wait()
    for i in range(2):
        fresh32[1 + i, 0:CAP, :] = fresh_in[:, i, :].astype(F32)
    count = cnt_in[0, 0]
    token = lax.broadcasted_iota(jnp.int32, (TOK, HD), 0)
    hits = []
    for c in range(CAP):
        used = jnp.full((TOK, HD), c, jnp.int32) < count
        hits.append((token == rows_in[0, c]) & used)

    def merged(h, i):
        rows = cached_in[i, :, lanes(h)].astype(F32)
        for c in range(CAP):
            rows = jnp.where(hits[c], fresh32[1 + i, c:c + 1, lanes(h)], rows)
        return rows.astype(BF16)

    for place in NEAR_FIRST:
        for i in range(2):
            kv_out[KV_SLOT[place], i * TOK:(i + 1) * TOK, :] = merged(head_of(*place), i)
        z_send(kv_out, kv_all.at[0], kz_s, kz_r, KV_SLOT, place)
    for i in range(2):
        kv_all[0, KV_SLOT[0, 0], i * TOK:(i + 1) * TOK, :] = merged(head_of(0, 0), i)

    loads[5].start()
    send(w_hbm, w_all.at[1], w_s, w_r, at_z(0, 1)).start()

    for t, half in enumerate((zl, 1 - zl, 0, 1)):
        first = t * 4 + (t * 4 == Q_SLOT[0, 0])
        arrived(q_land.at[first:t * 4 + 4], qz_r.at[t])
        packed = q_land[t * 4:(t + 1) * 4].astype(F32)[:, 0:8, :].reshape(32, HD)
        part = slice(t // 2 * 32, t // 2 * 32 + 32)
        q_all[half, 7, part, :] = packed.astype(BF16)
        for p in range(7):
            send(
                q_all.at[half, 7, part], q_all.at[half, p, part], qy_s, qy_r.at[p // 4], at_y(ORDER[p])
            ).start()
    for g in range(4):
        first = g * 4 + (g * 4 == KV_SLOT[0, 0])
        arrived(kv_all.at[0, first:g * 4 + 4], kz_r.at[g])
        part = slice(g * 4, g * 4 + 4)
        for s in (2, 1, 3):
            send(kv_all.at[0, part], kv_all.at[s, part], kx_s, kx_r.at[g], at_x(s)).start()

    tokens = NX * 4 * TOK
    vt[HD:HD + 16, :] = jnp.ones((16, tokens), BF16)

    def attend(keys, unit, first):
        queries = q_all[unit // 2, unit % 2 * 4:unit % 2 * 4 + 4].reshape(2 * HD, HD)
        scores = lax.dot_general(keys, queries, (((1,), (1,)), ((), ())), preferred_element_type=F32)
        top = jnp.max(scores, axis=0, keepdims=True) * SCALE2
        if not first:
            old = top_ref[unit]
            top = jnp.maximum(top, old)
        weights = jnp.exp2(scores * SCALE2 - top).astype(BF16)
        mixed = jnp.dot(vt[...], weights, preferred_element_type=F32)
        if not first:
            mixed = mixed + mix_ref[unit] * jnp.exp2(old - top)
        return top, mixed

    def own(p, g):
        return p == 7 and g == 2

    for g in range(4):
        part = slice(g * 4, g * 4 + 4)
        arrived(kv_all.at[1:4, part], kx_r.at[g])
        keys = kv_all[:, part, 0:TOK, :].reshape(tokens, HD)
        vt[0:HD, :] = kv_all[:, part, TOK:2 * TOK, :].reshape(tokens, HD).astype(F32).T.astype(BF16)
        for unit in (1, 3, 0, 2) if g == 0 else (0, 1, 2, 3):
            if g == 0 and unit == 1:
                arrived(q_all.at[:, 4:7], qy_r.at[1])
            if g == 0 and unit == 0:
                arrived(q_all.at[:, 0:4], qy_r.at[0])
            top, mixed = attend(keys, unit, g == 0)
            if g < 3:
                top_ref[unit] = top
                mix_ref[unit] = mixed
                continue
            i, base = unit // 2, unit % 2 * 4
            total = mixed[HD:HD + 1, :]
            level = top + jnp.log2(total)
            rows = (mixed[0:HD, :] * (1.0 / total)).T.astype(BF16)
            for n in range(2):
                st_out[i, base // 2 + n] = level[:, n * HD:(n + 1) * HD]
            o_out[i, base:base + 4] = rows.reshape(4, 64, HD)
            for p in range(base, base + 4):
                for k in range(4):
                    if not own(p, k):
                        dev = at_o(NY - ORDER[p], k < 2, k % 2)
                        send(st_out.at[i, p // 2], st_in.at[i, k, p], t_s.at[i, k], t_r.at[i, k], dev).start()
                        piece = o_out.at[i, p, k * 16:(k + 1) * 16]
                        send(piece, o_in.at[i, k, p], o_s.at[i, k], o_r.at[i, k], dev).start()

    row8 = lax.broadcasted_iota(jnp.int32, (8, HD), 0)
    lane8 = lax.broadcasted_iota(jnp.int32, (8, HD), 1)
    row = lax.broadcasted_iota(jnp.int32, (16, HD), 0)
    lane = lax.broadcasted_iota(jnp.int32, (16, HD), 1)
    straight = rem(lane, 16) == row
    swapped = rem(lane, 16) == rem(row + 8, 16)
    valid = lax.broadcasted_iota(jnp.int32, (8, CW), 0) < count
    for i in range(2):
        st_in[i, 2, 7] = st_out[i, 3]
        o_in[i, 2, 7] = o_out[i, 7, 32:48]
        levels = []
        for k in range(4):
            arrived(st_in.at[i, k, 0:8 - (k == 2)], t_r.at[i, k])
            seen = jnp.concatenate([st_in[i, k, p] for p in range(NY)], axis=0)
            seen = pltpu.roll(seen, 0, 1, stride=16, stride_axis=0)
            low, high = (pltpu.roll(seen, (HD + shift - k * 16) % HD, 1) for shift in (0, 64))
            moved = jnp.where(rem(row8, 2) == 0, low, high)
            levels.append(jnp.sum(jnp.where(div(lane8, 16) == row8, moved, 0.0), axis=0, keepdims=True))
        levels = jnp.concatenate(levels + levels, axis=0)
        peak = levels
        for shift in (16, 32, 64):
            peak = jnp.maximum(peak, pltpu.roll(peak, shift, 1))
        parts = jnp.exp2(levels - peak)
        total = parts
        for shift in (16, 32, 64):
            total = total + pltpu.roll(total, shift, 1)
        shares = parts / total

        mean = []
        for k in range(4):
            arrived(o_in.at[i, k, 0:8 - (k == 2)], o_r.at[i, k])
            mix = jnp.where(straight, shares[k:k + 1, :], 0.0)
            if k < 2 and i == 0:
                mix = jnp.where(zl == 1, mix, jnp.where(swapped, shares[k:k + 1, :], 0.0))
            mean.append(jnp.dot(mix.astype(BF16), o_in[i, k].reshape(HD, HD), preferred_element_type=F32))
        heads4 = [jnp.where(zl == z, mean[2 + dc], mean[dc]) for dc in range(2) for z in range(2)]
        rows = jnp.concatenate(heads4, axis=1).astype(BF16)

        if i == 0:
            loads[5].wait()
            send(w_hbm, w_all.at[1], w_s, w_r, at_z(0, 1)).wait_recv()
        for ci in range(CHUNKS):
            sides = []
            for start in (ci * CW, HALF + ci * CW):
                w = jnp.concatenate([w_all[0, :, start:start + CW], w_all[1, :, start:start + CW]], axis=0)
                sides.append(jnp.dot(rows, w, preferred_element_type=F32))
            for n in range(2):
                b = n * 2 + i
                block = jnp.concatenate([side[n * 8:(n + 1) * 8] for side in sides], axis=0)
                p_out[b, ci] = block.astype(BF16)
                if b:
                    send(p_out.at[b, ci], p_in.at[b, ci], p_s.at[b], p_r.at[b], at_p(b)).start()

    for b in (2, 1, 3):
        arrived(p_in.at[b], p_r.at[b])
    for ci in range(CHUNKS):
        total = p_out[0, ci].astype(F32)
        for b in (1, 3, 2):
            total = total + p_in[b, ci].astype(F32)
        out_ref[:, ci * CW:(ci + 1) * CW] = jnp.where(valid, total[0:8], 0.0)
        out_ref[:, HALF + ci * CW:HALF + (ci + 1) * CW] = jnp.where(valid, total[8:16], 0.0)

    left(q_out.at[0:15], qz_s)
    left(kv_out.at[0:15], kz_s)
    send(w_hbm, w_all.at[1], w_s, w_r, at_z(0, 1)).wait_send()
    left(q_all.at[:, 0:7], qy_s)
    left(kv_all.at[1:4], kx_s)
    for i in range(2):
        for k in range(4):
            left(st_in.at[i, k, 0:8 - (k == 2)], t_s.at[i, k])
            left(o_in.at[i, k, 0:8 - (k == 2)], o_s.at[i, k])
    for b in range(1, NZ):
        left(p_out.at[b], p_s.at[b])


def on_device(fresh_query, fresh_entries, cached_entries, recompute_rows, valid_counts, out_weight, out_gate):
    dma = pltpu.SemaphoreType.DMA
    width = HEADS * HD
    summed = pl.pallas_call(
        kernel,
        out_shape=pltpu.VMEM((8, D), F32),
        in_specs=[pl.BlockSpec(memory_space=pl.ANY)] * 6,
        out_specs=pl.BlockSpec(memory_space=pltpu.VMEM),
        scratch_shapes=[
            pltpu.VMEM((CAP, width), BF16),
            pltpu.VMEM((CAP, 2, width), BF16),
            pltpu.VMEM((2, TOK, width), BF16),
            pltpu.SMEM((1, CAP), jnp.int32),
            pltpu.SMEM((1, 1), jnp.int32),
            pltpu.VMEM((3, 8, width), F32),
            pltpu.VMEM((HEADS, 16, HD), BF16),
            pltpu.VMEM((HEADS, 2 * TOK, HD), BF16),
            pltpu.VMEM((HEADS, 16, HD), BF16),
            pltpu.VMEM((NX, HEADS, 2 * TOK, HD), BF16),
            pltpu.VMEM((2, NY, 64, HD), BF16),
            pltpu.VMEM((HD + 16, HEADS * TOK), BF16),
            pltpu.VMEM((4, 1, 2 * HD), F32),
            pltpu.VMEM((4, HD + 16, 2 * HD), F32),
            pltpu.VMEM((2, NY, 64, HD), BF16),
            pltpu.VMEM((2, 4, NY, 16, HD), BF16),
            pltpu.VMEM((2, 4, 1, HD), F32),
            pltpu.VMEM((2, 4, NY, 1, HD), F32),
            pltpu.VMEM((2, 2 * HD, D), BF16),
            pltpu.VMEM((NZ, CHUNKS, 16, CW), BF16),
            pltpu.VMEM((NZ, CHUNKS, 16, CW), BF16),
            dma((6,)),
            dma, dma((4,)), dma, dma((4,)),
            dma, dma,
            dma, dma((2,)),
            dma, dma((4,)),
            dma((2, 4)), dma((2, 4)), dma((2, 4)), dma((2, 4)),
            dma((NZ,)), dma((NZ,)),
        ],
        compiler_params=pltpu.CompilerParams(
            collective_id=0, has_side_effects=True, vmem_limit_bytes=60 * 1024 * 1024
        ),
    )(fresh_query, fresh_entries.transpose(1, 0, 2), cached_entries, recompute_rows, valid_counts.reshape(1, 1), out_weight)
    return (summed[:CAP] * out_gate[None, :]).astype(BF16)


def solution(mesh):
    both = ("head", "blk")
    in_specs = (P(both, None), P(None, both, None), P(None, both, None), P(both, None), P(both), P("head", None), P())
    return jax.shard_map(on_device, mesh=mesh, in_specs=in_specs, out_specs=P(both, None), check_vma=False)
```

```python
import functools
import math

import jax
import jax.numpy as jnp
from jax import lax
from jax.experimental import pallas as pl
from jax.experimental.pallas import tpu as pltpu
from jax.sharding import PartitionSpec as P

HD = 128
HEADS = 16
TOK = 16
CAP = 7
D = 3072
NX, NY, NZ, CHIPS = 4, 8, 4, 8
CHUNKS = 3
HALF = D // 2
CW = HALF // CHUNKS
SCALE2 = (HD ** -0.5) * math.log2(math.e)
MESH = pl.DeviceIdType.MESH
F32, BF16 = jnp.float32, jnp.bfloat16

PLACES = [(dz, dc) for dz in range(CHIPS) for dc in range(2)]


def slots(groups):
    return {(dz, dc): g * 4 + dc * 2 + e for g, pair in enumerate(groups) for e, dz in enumerate(pair) for dc in range(2)}


KV_SLOT = slots(((1, 7), (2, 6), (3, 5), (0, 4)))
Q_SLOT = slots(((1, 5), (3, 7), (0, 4), (2, 6)))
NEAR_FIRST = sorted((k for k in PLACES if k != (0, 0)), key=lambda k: min(k[0], CHIPS - k[0]))
FAR_FIRST = NEAR_FIRST[::-1]
ORDER = (4, 3, 5, 2, 6, 1, 7, 0)


def kernel(
    q_hbm, fresh_hbm, cached_hbm, rows_hbm, cnt_hbm, w_hbm, out_ref,
    q_in, fresh_in, cached_in, rows_in, cnt_in, fresh32, q_out, kv_out, q_land, kv_all, q_all, vt,
    o_out, o_in, st_out, st_in, w_all, p_out, p_in,
    sem_in, qz_s, qz_r, kz_s, kz_r, w_s, w_r, qy_s, qy_r, kx_s, kx_r, o_s, o_r, t_s, t_r, p_s, p_r,
):
    head = lax.axis_index("head")
    blk = lax.axis_index("blk")

    def div(a, b):
        return lax.div(a, jnp.int32(b))

    def rem(a, b):
        return lax.rem(a, jnp.int32(b))

    core, zh = rem(head, 2), div(head, 2)
    y, zl, x = rem(blk, NY), rem(div(blk, NY), 2), div(blk, 2 * NY)
    chip = zh * 2 + zl
    ups = [rem(chip + dz, CHIPS) for dz in range(CHIPS)]
    cores = [core, 1 - core]

    def at_z(dz, dc):
        return (div(ups[dz], 2) * 2 + cores[dc], (x * 2 + rem(ups[dz], 2)) * NY + y)

    def head_of(dz, dc):
        return div(ups[dz], 2) * 4 + cores[dc] * 2 + rem(ups[dz], 2)

    def at_x(dx):
        return (head, (rem(x + dx, NX) * 2 + zl) * NY + y)

    def at_y(dy):
        return (head, (x * 2 + zl) * NY + rem(y + dy, NY))

    def at_o(dy, odd, dc):
        return (zh * 2 + cores[dc], (x * 2 + (1 - zl if odd else zl)) * NY + rem(y + dy, NY))

    def at_p(b):
        return (rem(zh + b, NZ) * 2 + core, blk)

    def send(src, dst, s_sem, r_sem, dev):
        return pltpu.make_async_remote_copy(
            src_ref=src, dst_ref=dst, send_sem=s_sem, recv_sem=r_sem,
            device_id=dev, device_id_type=MESH,
        )

    def arrived(ref, sem):
        send(ref, ref, sem, sem, at_x(1)).wait_recv()

    def left(ref, sem):
        send(ref, ref, sem, sem, at_x(1)).wait_send()

    loads = [
        pltpu.make_async_copy(q_hbm, q_in, sem_in.at[0]),
        pltpu.make_async_copy(fresh_hbm, fresh_in, sem_in.at[1]),
        pltpu.make_async_copy(cached_hbm, cached_in, sem_in.at[2]),
        pltpu.make_async_copy(rows_hbm, rows_in, sem_in.at[3]),
        pltpu.make_async_copy(cnt_hbm, cnt_in, sem_in.at[4]),
        pltpu.make_async_copy(w_hbm, w_all.at[0], sem_in.at[5]),
    ]
    barrier = pltpu.get_barrier_semaphore()
    partners = [at_z(dz, dc) for dz, dc in FAR_FIRST]
    partners += [at_y(dy) for dy in ORDER[:7]] + [at_x(dx) for dx in (2, 1, 3)]
    for dev in partners:
        pl.semaphore_signal(barrier, inc=1, device_id=dev, device_id_type=MESH)
    for load in loads[:5]:
        load.start()

    fresh32[0, ...] = jnp.zeros((8, HEADS * HD), F32)
    loads[0].wait()
    fresh32[0, 0:CAP, :] = q_in[...].astype(F32)

    def lanes(h):
        return pl.ds(pl.multiple_of(h * HD, HD), HD)

    for place in [(0, 0)] + FAR_FIRST:
        rows8 = fresh32[0, :, lanes(head_of(*place))]
        q_out[Q_SLOT[place]] = jnp.concatenate([rows8, jnp.zeros((8, HD), F32)], axis=0).astype(BF16)
    q_land[Q_SLOT[0, 0]] = q_out[Q_SLOT[0, 0]]
    pl.semaphore_wait(barrier, len(partners))

    def z_send(out, land, s_sem, r_sem, table, place):
        back = table[(CHIPS - place[0]) % CHIPS, place[1]]
        send(out.at[table[place]], land.at[back], s_sem, r_sem.at[back // 4], at_z(*place)).start()

    for place in FAR_FIRST:
        z_send(q_out, q_land, qz_s, qz_r, Q_SLOT, place)

    for i in (1, 2, 3, 4):
        loads[i].wait()
    for i in range(2):
        fresh32[1 + i, 0:CAP, :] = fresh_in[:, i, :].astype(F32)
    count = cnt_in[0, 0]
    token = lax.broadcasted_iota(jnp.int32, (TOK, HD), 0)
    hits = []
    for c in range(CAP):
        used = jnp.full((TOK, HD), c, jnp.int32) < count
        hits.append((token == rows_in[0, c]) & used)

    def merged(h, i):
        rows = cached_in[i, :, lanes(h)].astype(F32)
        for c in range(CAP):
            rows = jnp.where(hits[c], fresh32[1 + i, c:c + 1, lanes(h)], rows)
        return rows.astype(BF16)

    for place in NEAR_FIRST:
        for i in range(2):
            kv_out[KV_SLOT[place], i * TOK:(i + 1) * TOK, :] = merged(head_of(*place), i)
        z_send(kv_out, kv_all.at[0], kz_s, kz_r, KV_SLOT, place)
    for i in range(2):
        kv_all[0, KV_SLOT[0, 0], i * TOK:(i + 1) * TOK, :] = merged(head_of(0, 0), i)

    loads[5].start()
    send(w_hbm, w_all.at[1], w_s, w_r, at_z(0, 1)).start()

    def pass_queries(t):
        half = (zl, 1 - zl, 0, 1)[t]
        first = t * 4 + (t * 4 == Q_SLOT[0, 0])
        arrived(q_land.at[first:t * 4 + 4], qz_r.at[t])
        packed = q_land[t * 4:(t + 1) * 4].astype(F32)[:, 0:8, :].reshape(32, HD)
        part = slice(t // 2 * 32, t // 2 * 32 + 32)
        q_all[half, 7, part, :] = packed.astype(BF16)
        for p in range(7):
            send(
                q_all.at[half, 7, part], q_all.at[half, p, part], qy_s, qy_r.at[p // 4], at_y(ORDER[p])
            ).start()

    def pass_entries(g):
        first = g * 4 + (g * 4 == KV_SLOT[0, 0])
        arrived(kv_all.at[0, first:g * 4 + 4], kz_r.at[g])
        part = slice(g * 4, g * 4 + 4)
        for s in (2, 1, 3):
            send(kv_all.at[0, part], kv_all.at[s, part], kx_s, kx_r.at[g], at_x(s)).start()

    pass_queries(3)
    pass_entries(0)
    pass_queries(0)
    pass_queries(1)
    pass_entries(1)
    pass_entries(2)
    pass_queries(2)
    pass_entries(3)

    group = NX * 4 * TOK
    for g in range(4):
        part = slice(g * 4, g * 4 + 4)
        arrived(kv_all.at[1:4, part], kx_r.at[g])
        values = kv_all[:, part, TOK:2 * TOK, :].reshape(group, HD)
        vt[0:HD, g * group:(g + 1) * group] = values.astype(F32).T.astype(BF16)
    vt[HD:HD + 16, :] = jnp.ones((16, 4 * group), BF16)

    def own(p, g):
        return p == 7 and g == 2

    for near in (1, 0):
        arrived(q_all.at[:, near * 4:near * 4 + 4 - near], qy_r.at[near])
    for unit in range(4):
        keys = jnp.concatenate(
            [kv_all[:, g * 4:g * 4 + 4, 0:TOK, :].reshape(group, HD) for g in range(4)], axis=0
        )
        queries = q_all[unit // 2, unit % 2 * 4:unit % 2 * 4 + 4].reshape(2 * HD, HD)
        scores = lax.dot_general(keys, queries, (((1,), (1,)), ((), ())), preferred_element_type=F32)
        top = jnp.max(scores, axis=0, keepdims=True) * SCALE2
        weights = jnp.exp2(scores * SCALE2 - top).astype(BF16)
        mixed = jnp.dot(vt[...], weights, preferred_element_type=F32)
        i, base = unit // 2, unit % 2 * 4
        total = mixed[HD:HD + 1, :]
        level = top + jnp.log2(total)
        rows = (mixed[0:HD, :] * (1.0 / total)).T.astype(BF16)
        for n in range(2):
            st_out[i, base // 2 + n] = level[:, n * HD:(n + 1) * HD]
        o_out[i, base:base + 4] = rows.reshape(4, 64, HD)
        for p in range(base, base + 4):
            for k in range(4):
                if not own(p, k):
                    dev = at_o(NY - ORDER[p], k < 2, k % 2)
                    send(st_out.at[i, p // 2], st_in.at[i, k, p], t_s.at[i, k], t_r.at[i, k], dev).start()
                    piece = o_out.at[i, p, k * 16:(k + 1) * 16]
                    send(piece, o_in.at[i, k, p], o_s.at[i, k], o_r.at[i, k], dev).start()

    row8 = lax.broadcasted_iota(jnp.int32, (8, HD), 0)
    lane8 = lax.broadcasted_iota(jnp.int32, (8, HD), 1)
    row = lax.broadcasted_iota(jnp.int32, (16, HD), 0)
    lane = lax.broadcasted_iota(jnp.int32, (16, HD), 1)
    straight = rem(lane, 16) == row
    swapped = rem(lane, 16) == rem(row + 8, 16)
    valid = lax.broadcasted_iota(jnp.int32, (8, CW), 0) < count
    for i in range(2):
        st_in[i, 2, 7] = st_out[i, 3]
        o_in[i, 2, 7] = o_out[i, 7, 32:48]
        levels = []
        for k in range(4):
            arrived(st_in.at[i, k, 0:8 - (k == 2)], t_r.at[i, k])
            seen = jnp.concatenate([st_in[i, k, p] for p in range(NY)], axis=0)
            seen = pltpu.roll(seen, 0, 1, stride=16, stride_axis=0)
            low, high = (pltpu.roll(seen, (HD + shift - k * 16) % HD, 1) for shift in (0, 64))
            moved = jnp.where(rem(row8, 2) == 0, low, high)
            levels.append(jnp.sum(jnp.where(div(lane8, 16) == row8, moved, 0.0), axis=0, keepdims=True))
        levels = jnp.concatenate(levels + levels, axis=0)
        peak = levels
        for shift in (16, 32, 64):
            peak = jnp.maximum(peak, pltpu.roll(peak, shift, 1))
        parts = jnp.exp2(levels - peak)
        total = parts
        for shift in (16, 32, 64):
            total = total + pltpu.roll(total, shift, 1)
        shares = parts / total

        mean = []
        for k in range(4):
            arrived(o_in.at[i, k, 0:8 - (k == 2)], o_r.at[i, k])
            mix = jnp.where(straight, shares[k:k + 1, :], 0.0)
            if k < 2 and i == 0:
                mix = jnp.where(zl == 1, mix, jnp.where(swapped, shares[k:k + 1, :], 0.0))
            mean.append(jnp.dot(mix.astype(BF16), o_in[i, k].reshape(HD, HD), preferred_element_type=F32))
        heads4 = [jnp.where(zl == z, mean[2 + dc], mean[dc]) for dc in range(2) for z in range(2)]
        rows = jnp.concatenate(heads4, axis=1).astype(BF16)

        if i == 0:
            loads[5].wait()
            send(w_hbm, w_all.at[1], w_s, w_r, at_z(0, 1)).wait_recv()
        for ci in range(CHUNKS):
            sides = []
            for start in (ci * CW, HALF + ci * CW):
                w = jnp.concatenate([w_all[0, :, start:start + CW], w_all[1, :, start:start + CW]], axis=0)
                sides.append(jnp.dot(rows, w, preferred_element_type=F32))
            for n in range(2):
                b = n * 2 + i
                block = jnp.concatenate([side[n * 8:(n + 1) * 8] for side in sides], axis=0)
                p_out[b, ci] = block.astype(BF16)
                if b:
                    send(p_out.at[b, ci], p_in.at[b, ci], p_s.at[b], p_r.at[b], at_p(b)).start()

    for b in (2, 1, 3):
        arrived(p_in.at[b], p_r.at[b])
    for ci in range(CHUNKS):
        total = p_out[0, ci].astype(F32)
        for b in (1, 3, 2):
            total = total + p_in[b, ci].astype(F32)
        out_ref[:, ci * CW:(ci + 1) * CW] = jnp.where(valid, total[0:8], 0.0)
        out_ref[:, HALF + ci * CW:HALF + (ci + 1) * CW] = jnp.where(valid, total[8:16], 0.0)

    left(q_out.at[0:15], qz_s)
    left(kv_out.at[0:15], kz_s)
    send(w_hbm, w_all.at[1], w_s, w_r, at_z(0, 1)).wait_send()
    left(q_all.at[:, 0:7], qy_s)
    left(kv_all.at[1:4], kx_s)
    for i in range(2):
        for k in range(4):
            left(st_in.at[i, k, 0:8 - (k == 2)], t_s.at[i, k])
            left(o_in.at[i, k, 0:8 - (k == 2)], o_s.at[i, k])
    for b in range(1, NZ):
        left(p_out.at[b], p_s.at[b])


def on_device(fresh_query, fresh_entries, cached_entries, recompute_rows, valid_counts, out_weight, out_gate):
    dma = pltpu.SemaphoreType.DMA
    width = HEADS * HD
    summed = pl.pallas_call(
        kernel,
        out_shape=pltpu.VMEM((8, D), F32),
        in_specs=[pl.BlockSpec(memory_space=pl.ANY)] * 6,
        out_specs=pl.BlockSpec(memory_space=pltpu.VMEM),
        scratch_shapes=[
            pltpu.VMEM((CAP, width), BF16),
            pltpu.VMEM((CAP, 2, width), BF16),
            pltpu.VMEM((2, TOK, width), BF16),
            pltpu.SMEM((1, CAP), jnp.int32),
            pltpu.SMEM((1, 1), jnp.int32),
            pltpu.VMEM((3, 8, width), F32),
            pltpu.VMEM((HEADS, 16, HD), BF16),
            pltpu.VMEM((HEADS, 2 * TOK, HD), BF16),
            pltpu.VMEM((HEADS, 16, HD), BF16),
            pltpu.VMEM((NX, HEADS, 2 * TOK, HD), BF16),
            pltpu.VMEM((2, NY, 64, HD), BF16),
            pltpu.VMEM((HD + 16, 4 * HEADS * TOK), BF16),
            pltpu.VMEM((2, NY, 64, HD), BF16),
            pltpu.VMEM((2, 4, NY, 16, HD), BF16),
            pltpu.VMEM((2, 4, 1, HD), F32),
            pltpu.VMEM((2, 4, NY, 1, HD), F32),
            pltpu.VMEM((2, 2 * HD, D), BF16),
            pltpu.VMEM((NZ, CHUNKS, 16, CW), BF16),
            pltpu.VMEM((NZ, CHUNKS, 16, CW), BF16),
            dma((6,)),
            dma, dma((4,)), dma, dma((4,)),
            dma, dma,
            dma, dma((2,)),
            dma, dma((4,)),
            dma((2, 4)), dma((2, 4)), dma((2, 4)), dma((2, 4)),
            dma((NZ,)), dma((NZ,)),
        ],
        compiler_params=pltpu.CompilerParams(
            collective_id=0, has_side_effects=True, vmem_limit_bytes=60 * 1024 * 1024
        ),
    )(fresh_query, fresh_entries.transpose(1, 0, 2), cached_entries, recompute_rows, valid_counts.reshape(1, 1), out_weight)
    return (summed[:CAP] * out_gate[None, :]).astype(BF16)


def solution(mesh):
    both = ("head", "blk")
    in_specs = (P(both, None), P(None, both, None), P(None, both, None), P(both, None), P(both), P("head", None), P())
    return jax.shard_map(on_device, mesh=mesh, in_specs=in_specs, out_specs=P(both, None), check_vma=False)
```

```python
import functools
import math

import jax
import jax.numpy as jnp
from jax import lax
from jax.experimental import pallas as pl
from jax.experimental.pallas import tpu as pltpu
from jax.sharding import PartitionSpec as P

HD = 128
HEADS = 16
TOK = 16
CAP = 7
D = 3072
NX, NY, NZ, CHIPS = 4, 8, 4, 8
CHUNKS = 3
HALF = D // 2
CW = HALF // CHUNKS
SCALE2 = (HD ** -0.5) * math.log2(math.e)
MESH = pl.DeviceIdType.MESH
F32, BF16 = jnp.float32, jnp.bfloat16

PLACES = [(dz, dc) for dz in range(CHIPS) for dc in range(2)]


def slots(groups):
    return {(dz, dc): g * 4 + dc * 2 + e for g, pair in enumerate(groups) for e, dz in enumerate(pair) for dc in range(2)}


KV_SLOT = slots(((1, 7), (2, 6), (3, 5), (0, 4)))
Q_SLOT = slots(((1, 5), (3, 7), (0, 4), (2, 6)))
NEAR_FIRST = sorted((k for k in PLACES if k != (0, 0)), key=lambda k: min(k[0], CHIPS - k[0]))
FAR_FIRST = NEAR_FIRST[::-1]
ORDER = (4, 3, 5, 2, 6, 1, 7, 0)


def kernel(
    q_hbm, fresh_hbm, cached_hbm, rows_hbm, cnt_hbm, w_hbm, out_ref,
    q_in, fresh_in, cached_in, rows_in, cnt_in, fresh32, q_out, kv_out, q_land, kv_all, q_all, vt,
    o_out, o_in, st_out, st_in, w_all, p_out, p_in,
    sem_in, qz_s, qz_r, kz_s, kz_r, w_s, w_r, qy_s, qy_r, kx_s, kx_r, o_s, o_r, t_s, t_r, p_s, p_r,
):
    head = lax.axis_index("head")
    blk = lax.axis_index("blk")

    def div(a, b):
        return lax.div(a, jnp.int32(b))

    def rem(a, b):
        return lax.rem(a, jnp.int32(b))

    core, zh = rem(head, 2), div(head, 2)
    y, zl, x = rem(blk, NY), rem(div(blk, NY), 2), div(blk, 2 * NY)
    chip = zh * 2 + zl
    ups = [rem(chip + dz, CHIPS) for dz in range(CHIPS)]
    cores = [core, 1 - core]

    def at_z(dz, dc):
        return (div(ups[dz], 2) * 2 + cores[dc], (x * 2 + rem(ups[dz], 2)) * NY + y)

    def head_of(dz, dc):
        return div(ups[dz], 2) * 4 + cores[dc] * 2 + rem(ups[dz], 2)

    def at_x(dx):
        return (head, (rem(x + dx, NX) * 2 + zl) * NY + y)

    def at_y(dy):
        return (head, (x * 2 + zl) * NY + rem(y + dy, NY))

    def at_o(dy, odd, dc):
        return (zh * 2 + cores[dc], (x * 2 + (1 - zl if odd else zl)) * NY + rem(y + dy, NY))

    def at_p(b):
        return (rem(zh + b, NZ) * 2 + core, blk)

    def send(src, dst, s_sem, r_sem, dev):
        return pltpu.make_async_remote_copy(
            src_ref=src, dst_ref=dst, send_sem=s_sem, recv_sem=r_sem,
            device_id=dev, device_id_type=MESH,
        )

    def arrived(ref, sem):
        send(ref, ref, sem, sem, at_x(1)).wait_recv()

    def left(ref, sem):
        send(ref, ref, sem, sem, at_x(1)).wait_send()

    loads = [
        pltpu.make_async_copy(q_hbm, q_in, sem_in.at[0]),
        pltpu.make_async_copy(fresh_hbm, fresh_in, sem_in.at[1]),
        pltpu.make_async_copy(cached_hbm, cached_in, sem_in.at[2]),
        pltpu.make_async_copy(rows_hbm, rows_in, sem_in.at[3]),
        pltpu.make_async_copy(cnt_hbm, cnt_in, sem_in.at[4]),
        pltpu.make_async_copy(w_hbm, w_all.at[0], sem_in.at[5]),
    ]
    barrier = pltpu.get_barrier_semaphore()
    partners = [at_z(dz, dc) for dz, dc in FAR_FIRST]
    partners += [at_y(dy) for dy in ORDER[:7]] + [at_x(dx) for dx in (2, 1, 3)]
    for dev in partners[:15]:
        pl.semaphore_signal(barrier, inc=1, device_id=dev, device_id_type=MESH)
    for load in loads[:5]:
        load.start()
    for dev in partners[15:]:
        pl.semaphore_signal(barrier, inc=1, device_id=dev, device_id_type=MESH)

    fresh32[0, ...] = jnp.zeros((8, HEADS * HD), F32)
    loads[0].wait()
    fresh32[0, 0:CAP, :] = q_in[...].astype(F32)

    def lanes(h):
        return pl.ds(pl.multiple_of(h * HD, HD), HD)

    for place in [(0, 0)] + FAR_FIRST:
        rows8 = fresh32[0, :, lanes(head_of(*place))]
        q_out[Q_SLOT[place]] = jnp.concatenate([rows8, jnp.zeros((8, HD), F32)], axis=0).astype(BF16)
    q_land[Q_SLOT[0, 0]] = q_out[Q_SLOT[0, 0]]

    def z_send(out, land, s_sem, r_sem, table, place):
        back = table[(CHIPS - place[0]) % CHIPS, place[1]]
        send(out.at[table[place]], land.at[back], s_sem, r_sem.at[back // 4], at_z(*place)).start()

    for i in (1, 2, 3, 4):
        loads[i].wait()
    for i in range(2):
        fresh32[1 + i, 0:CAP, :] = fresh_in[:, i, :].astype(F32)
    count = cnt_in[0, 0]
    token = lax.broadcasted_iota(jnp.int32, (TOK, HD), 0)
    hits = []
    for c in range(CAP):
        used = jnp.full((TOK, HD), c, jnp.int32) < count
        hits.append((token == rows_in[0, c]) & used)

    def merged(h, i):
        rows = cached_in[i, :, lanes(h)].astype(F32)
        for c in range(CAP):
            rows = jnp.where(hits[c], fresh32[1 + i, c:c + 1, lanes(h)], rows)
        return rows.astype(BF16)

    for place in PLACES:
        for i in range(2):
            kv_out[KV_SLOT[place], i * TOK:(i + 1) * TOK, :] = merged(head_of(*place), i)
    kv_all[0, KV_SLOT[0, 0]] = kv_out[KV_SLOT[0, 0]]

    pl.semaphore_wait(barrier, len(partners))
    for place in FAR_FIRST:
        z_send(q_out, q_land, qz_s, qz_r, Q_SLOT, place)
    for place in NEAR_FIRST:
        z_send(kv_out, kv_all.at[0], kz_s, kz_r, KV_SLOT, place)

    loads[5].start()
    send(w_hbm, w_all.at[1], w_s, w_r, at_z(0, 1)).start()

    def pass_queries(t):
        half = (zl, 1 - zl, 0, 1)[t]
        first = t * 4 + (t * 4 == Q_SLOT[0, 0])
        arrived(q_land.at[first:t * 4 + 4], qz_r.at[t])
        packed = q_land[t * 4:(t + 1) * 4].astype(F32)[:, 0:8, :].reshape(32, HD)
        part = slice(t // 2 * 32, t // 2 * 32 + 32)
        q_all[half, 7, part, :] = packed.astype(BF16)
        for p in range(7):
            send(
                q_all.at[half, 7, part], q_all.at[half, p, part], qy_s, qy_r.at[p // 4], at_y(ORDER[p])
            ).start()

    def pass_entries(g):
        first = g * 4 + (g * 4 == KV_SLOT[0, 0])
        arrived(kv_all.at[0, first:g * 4 + 4], kz_r.at[g])
        part = slice(g * 4, g * 4 + 4)
        for s in (2, 1, 3):
            send(kv_all.at[0, part], kv_all.at[s, part], kx_s, kx_r.at[g], at_x(s)).start()

    pass_queries(3)
    pass_entries(0)
    pass_queries(0)
    pass_queries(1)
    pass_entries(1)
    pass_entries(2)
    pass_queries(2)
    pass_entries(3)

    group = NX * 4 * TOK
    for g in range(4):
        part = slice(g * 4, g * 4 + 4)
        arrived(kv_all.at[1:4, part], kx_r.at[g])
        values = kv_all[:, part, TOK:2 * TOK, :].reshape(group, HD)
        vt[0:HD, g * group:(g + 1) * group] = values.astype(F32).T.astype(BF16)
    vt[HD:HD + 16, :] = jnp.ones((16, 4 * group), BF16)

    def own(p, g):
        return p == 7 and g == 2

    for near in (1, 0):
        arrived(q_all.at[:, near * 4:near * 4 + 4 - near], qy_r.at[near])
    for unit in range(4):
        keys = jnp.concatenate(
            [kv_all[:, g * 4:g * 4 + 4, 0:TOK, :].reshape(group, HD) for g in range(4)], axis=0
        )
        queries = q_all[unit // 2, unit % 2 * 4:unit % 2 * 4 + 4].reshape(2 * HD, HD)
        scores = lax.dot_general(keys, queries, (((1,), (1,)), ((), ())), preferred_element_type=F32)
        top = jnp.max(scores, axis=0, keepdims=True) * SCALE2
        weights = jnp.exp2(scores * SCALE2 - top).astype(BF16)
        mixed = jnp.dot(vt[...], weights, preferred_element_type=F32)
        i, base = unit // 2, unit % 2 * 4
        total = mixed[HD:HD + 1, :]
        level = top + jnp.log2(total)
        rows = (mixed[0:HD, :] * (1.0 / total)).T.astype(BF16)
        for n in range(2):
            st_out[i, base // 2 + n] = level[:, n * HD:(n + 1) * HD]
        o_out[i, base:base + 4] = rows.reshape(4, 64, HD)
        for p in range(base, base + 4):
            for k in range(4):
                if not own(p, k):
                    dev = at_o(NY - ORDER[p], k < 2, k % 2)
                    send(st_out.at[i, p // 2], st_in.at[i, k, p], t_s.at[i, k], t_r.at[i, k], dev).start()
        for p in range(base, base + 4):
            for k in range(4):
                if not own(p, k):
                    dev = at_o(NY - ORDER[p], k < 2, k % 2)
                    piece = o_out.at[i, p, k * 16:(k + 1) * 16]
                    send(piece, o_in.at[i, k, p], o_s.at[i, k], o_r.at[i, k], dev).start()

    row8 = lax.broadcasted_iota(jnp.int32, (8, HD), 0)
    lane8 = lax.broadcasted_iota(jnp.int32, (8, HD), 1)
    row = lax.broadcasted_iota(jnp.int32, (16, HD), 0)
    lane = lax.broadcasted_iota(jnp.int32, (16, HD), 1)
    straight = rem(lane, 16) == row
    swapped = rem(lane, 16) == rem(row + 8, 16)
    valid = lax.broadcasted_iota(jnp.int32, (8, CW), 0) < count
    for i in range(2):
        st_in[i, 2, 7] = st_out[i, 3]
        o_in[i, 2, 7] = o_out[i, 7, 32:48]
        levels = []
        for k in range(4):
            arrived(st_in.at[i, k, 0:8 - (k == 2)], t_r.at[i, k])
            seen = jnp.concatenate([st_in[i, k, p] for p in range(NY)], axis=0)
            seen = pltpu.roll(seen, 0, 1, stride=16, stride_axis=0)
            low, high = (pltpu.roll(seen, (HD + shift - k * 16) % HD, 1) for shift in (0, 64))
            moved = jnp.where(rem(row8, 2) == 0, low, high)
            levels.append(jnp.sum(jnp.where(div(lane8, 16) == row8, moved, 0.0), axis=0, keepdims=True))
        levels = jnp.concatenate(levels + levels, axis=0)
        peak = levels
        for shift in (16, 32, 64):
            peak = jnp.maximum(peak, pltpu.roll(peak, shift, 1))
        parts = jnp.exp2(levels - peak)
        total = parts
        for shift in (16, 32, 64):
            total = total + pltpu.roll(total, shift, 1)
        shares = parts / total

        mean = []
        for k in range(4):
            arrived(o_in.at[i, k, 0:8 - (k == 2)], o_r.at[i, k])
            mix = jnp.where(straight, shares[k:k + 1, :], 0.0)
            if k < 2 and i == 0:
                mix = jnp.where(zl == 1, mix, jnp.where(swapped, shares[k:k + 1, :], 0.0))
            mean.append(jnp.dot(mix.astype(BF16), o_in[i, k].reshape(HD, HD), preferred_element_type=F32))
        heads4 = [jnp.where(zl == z, mean[2 + dc], mean[dc]) for dc in range(2) for z in range(2)]
        rows = jnp.concatenate(heads4, axis=1).astype(BF16)

        if i == 0:
            loads[5].wait()
            send(w_hbm, w_all.at[1], w_s, w_r, at_z(0, 1)).wait_recv()
        for ci in range(CHUNKS):
            sides = []
            for start in (ci * CW, HALF + ci * CW):
                w = jnp.concatenate([w_all[0, :, start:start + CW], w_all[1, :, start:start + CW]], axis=0)
                sides.append(jnp.dot(rows, w, preferred_element_type=F32))
            for n in range(2):
                b = n * 2 + i
                block = jnp.concatenate([side[n * 8:(n + 1) * 8] for side in sides], axis=0)
                p_out[b, ci] = block.astype(BF16)
                if b:
                    send(p_out.at[b, ci], p_in.at[b, ci], p_s.at[b], p_r.at[b], at_p(b)).start()

    for b in (2, 1, 3):
        arrived(p_in.at[b], p_r.at[b])
    for ci in range(CHUNKS):
        total = p_out[0, ci].astype(F32)
        for b in (1, 3, 2):
            total = total + p_in[b, ci].astype(F32)
        out_ref[:, ci * CW:(ci + 1) * CW] = jnp.where(valid, total[0:8], 0.0)
        out_ref[:, HALF + ci * CW:HALF + (ci + 1) * CW] = jnp.where(valid, total[8:16], 0.0)

    left(q_out.at[0:15], qz_s)
    left(kv_out.at[0:15], kz_s)
    send(w_hbm, w_all.at[1], w_s, w_r, at_z(0, 1)).wait_send()
    left(q_all.at[:, 0:7], qy_s)
    left(kv_all.at[1:4], kx_s)
    for i in range(2):
        for k in range(4):
            left(st_in.at[i, k, 0:8 - (k == 2)], t_s.at[i, k])
            left(o_in.at[i, k, 0:8 - (k == 2)], o_s.at[i, k])
    for b in range(1, NZ):
        left(p_out.at[b], p_s.at[b])


def on_device(fresh_query, fresh_entries, cached_entries, recompute_rows, valid_counts, out_weight, out_gate):
    dma = pltpu.SemaphoreType.DMA
    width = HEADS * HD
    summed = pl.pallas_call(
        kernel,
        out_shape=pltpu.VMEM((8, D), F32),
        in_specs=[pl.BlockSpec(memory_space=pl.ANY)] * 6,
        out_specs=pl.BlockSpec(memory_space=pltpu.VMEM),
        scratch_shapes=[
            pltpu.VMEM((CAP, width), BF16),
            pltpu.VMEM((CAP, 2, width), BF16),
            pltpu.VMEM((2, TOK, width), BF16),
            pltpu.SMEM((1, CAP), jnp.int32),
            pltpu.SMEM((1, 1), jnp.int32),
            pltpu.VMEM((3, 8, width), F32),
            pltpu.VMEM((HEADS, 16, HD), BF16),
            pltpu.VMEM((HEADS, 2 * TOK, HD), BF16),
            pltpu.VMEM((HEADS, 16, HD), BF16),
            pltpu.VMEM((NX, HEADS, 2 * TOK, HD), BF16),
            pltpu.VMEM((2, NY, 64, HD), BF16),
            pltpu.VMEM((HD + 16, 4 * HEADS * TOK), BF16),
            pltpu.VMEM((2, NY, 64, HD), BF16),
            pltpu.VMEM((2, 4, NY, 16, HD), BF16),
            pltpu.VMEM((2, 4, 1, HD), F32),
            pltpu.VMEM((2, 4, NY, 1, HD), F32),
            pltpu.VMEM((2, 2 * HD, D), BF16),
            pltpu.VMEM((NZ, CHUNKS, 16, CW), BF16),
            pltpu.VMEM((NZ, CHUNKS, 16, CW), BF16),
            dma((6,)),
            dma, dma((4,)), dma, dma((4,)),
            dma, dma,
            dma, dma((2,)),
            dma, dma((4,)),
            dma((2, 4)), dma((2, 4)), dma((2, 4)), dma((2, 4)),
            dma((NZ,)), dma((NZ,)),
        ],
        compiler_params=pltpu.CompilerParams(
            collective_id=0, has_side_effects=True, vmem_limit_bytes=60 * 1024 * 1024
        ),
    )(fresh_query, fresh_entries.transpose(1, 0, 2), cached_entries, recompute_rows, valid_counts.reshape(1, 1), out_weight)
    return (summed[:CAP] * out_gate[None, :]).astype(BF16)


def solution(mesh):
    both = ("head", "blk")
    in_specs = (P(both, None), P(None, both, None), P(None, both, None), P(both, None), P(both), P("head", None), P())
    return jax.shard_map(on_device, mesh=mesh, in_specs=in_specs, out_specs=P(both, None), check_vma=False)
```

```python
import functools
import math

import jax
import jax.numpy as jnp
from jax import lax
from jax.experimental import pallas as pl
from jax.experimental.pallas import tpu as pltpu
from jax.sharding import PartitionSpec as P

HD = 128
HEADS = 16
TOK = 16
CAP = 7
D = 3072
NX, NY, CHIPS = 4, 8, 8
CHUNKS = 3
HALF = D // 2
CW = HALF // CHUNKS
SCALE2 = (HD ** -0.5) * math.log2(math.e)
MESH = pl.DeviceIdType.MESH
F32, BF16 = jnp.float32, jnp.bfloat16

PLACES = [(dz, dc) for dz in range(CHIPS) for dc in range(2)]


def slots(groups):
    return {(dz, dc): g * 4 + dc * 2 + e for g, pair in enumerate(groups) for e, dz in enumerate(pair) for dc in range(2)}


SLOT = slots(((1, 7), (2, 6), (3, 5), (0, 4)))
SELF = SLOT[0, 0]
NEAR_FIRST = sorted((k for k in PLACES if k != (0, 0)), key=lambda k: min(k[0], CHIPS - k[0]))
FAR_FIRST = NEAR_FIRST[::-1]
ORDER = (4, 3, 5, 2, 6, 1, 7, 0)


def kernel(
    q_hbm, fresh_hbm, cached_hbm, rows_hbm, cnt_hbm, w_hbm, out_ref,
    q_in, fresh_in, cached_in, rows_in, cnt_in, fresh32, q_out, kv_out, q_land, kv_all, q_row, q_all, vt,
    o_out, o_in, st_out, st_in, w_all, p_out, p_in,
    sem_in, qz_s, qz_r, kz_s, kz_r, w_s, w_r, qy_s, qy_r, kx_s, kx_r, o_s, o_r, t_s, t_r, p_s, p_r,
):
    head = lax.axis_index("head")
    blk = lax.axis_index("blk")

    def div(a, b):
        return lax.div(a, jnp.int32(b))

    def rem(a, b):
        return lax.rem(a, jnp.int32(b))

    core, zh = rem(head, 2), div(head, 2)
    y, zl, x = rem(blk, NY), rem(div(blk, NY), 2), div(blk, 2 * NY)
    chip = zh * 2 + zl
    cube, mine = div(zh, 2), rem(zh, 2)
    quarter = zl * 2 + core
    place_here = cube * 8 + quarter * 2 + mine
    ups = [rem(chip + dz, CHIPS) for dz in range(CHIPS)]
    cores = [core, 1 - core]

    def at_z(dz, dc):
        return (div(ups[dz], 2) * 2 + cores[dc], (x * 2 + rem(ups[dz], 2)) * NY + y)

    def head_of(dz, dc):
        return div(ups[dz], 2) * 4 + cores[dc] * 2 + rem(ups[dz], 2)

    def at_x(dx):
        return (head, (rem(x + dx, NX) * 2 + zl) * NY + y)

    def at_y(dy):
        return (head, (x * 2 + zl) * NY + rem(y + dy, NY))

    def at_o(dy, odd, dc):
        return (zh * 2 + cores[dc], (x * 2 + (1 - zl if odd else zl)) * NY + rem(y + dy, NY))

    def at_p(half, n):
        return ((half * 2 + n) * 2 + core, blk)

    def send(src, dst, s_sem, r_sem, dev):
        return pltpu.make_async_remote_copy(
            src_ref=src, dst_ref=dst, send_sem=s_sem, recv_sem=r_sem,
            device_id=dev, device_id_type=MESH,
        )

    def arrived(ref, sem):
        send(ref, ref, sem, sem, at_x(1)).wait_recv()

    def left(ref, sem):
        send(ref, ref, sem, sem, at_x(1)).wait_send()

    loads = [
        pltpu.make_async_copy(q_hbm, q_in, sem_in.at[0]),
        pltpu.make_async_copy(fresh_hbm, fresh_in, sem_in.at[1]),
        pltpu.make_async_copy(cached_hbm, cached_in, sem_in.at[2]),
        pltpu.make_async_copy(rows_hbm, rows_in, sem_in.at[3]),
        pltpu.make_async_copy(cnt_hbm, cnt_in, sem_in.at[4]),
        pltpu.make_async_copy(w_hbm, w_all.at[0], sem_in.at[5]),
    ]
    barrier = pltpu.get_barrier_semaphore()
    partners = [at_z(dz, dc) for dz, dc in FAR_FIRST]
    partners += [at_y(dy) for dy in ORDER[:7]] + [at_x(dx) for dx in (2, 1, 3)]
    for dev in partners[:15]:
        pl.semaphore_signal(barrier, inc=1, device_id=dev, device_id_type=MESH)
    for load in loads[:5]:
        load.start()
    for dev in partners[15:]:
        pl.semaphore_signal(barrier, inc=1, device_id=dev, device_id_type=MESH)

    fresh32[0, ...] = jnp.zeros((8, HEADS * HD), F32)
    loads[0].wait()
    fresh32[0, 0:CAP, :] = q_in[...].astype(F32)

    def lanes(h):
        return pl.ds(pl.multiple_of(h * HD, HD), HD)

    for place in [(0, 0)] + FAR_FIRST:
        rows8 = fresh32[0, :, lanes(head_of(*place))]
        q_out[SLOT[place]] = jnp.concatenate([rows8, jnp.zeros((8, HD), F32)], axis=0).astype(BF16)
    q_land[place_here] = q_out[SELF]

    pl.semaphore_wait(barrier, len(partners))
    for place in FAR_FIRST:
        apart = rem(div(ups[place[0]], 4) + cube, 2)
        send(q_out.at[SLOT[place]], q_land.at[place_here], qz_s, qz_r.at[apart], at_z(*place)).start()

    for i in (1, 2, 3, 4):
        loads[i].wait()
    for i in range(2):
        fresh32[1 + i, 0:CAP, :] = fresh_in[:, i, :].astype(F32)
    count = cnt_in[0, 0]
    token = lax.broadcasted_iota(jnp.int32, (TOK, HD), 0)
    hits = []
    for c in range(CAP):
        used = jnp.full((TOK, HD), c, jnp.int32) < count
        hits.append((token == rows_in[0, c]) & used)

    def merged(h, i):
        rows = cached_in[i, :, lanes(h)].astype(F32)
        for c in range(CAP):
            rows = jnp.where(hits[c], fresh32[1 + i, c:c + 1, lanes(h)], rows)
        return rows.astype(BF16)

    for place in PLACES:
        for i in range(2):
            kv_out[SLOT[place], i * TOK:(i + 1) * TOK, :] = merged(head_of(*place), i)
    kv_all[0, SELF] = kv_out[SELF]

    for place in NEAR_FIRST:
        back = SLOT[(CHIPS - place[0]) % CHIPS, place[1]]
        send(kv_out.at[SLOT[place]], kv_all.at[0, back], kz_s, kz_r.at[back // 4], at_z(*place)).start()

    loads[5].start()
    send(w_hbm, w_all.at[1], w_s, w_r, at_z(0, 1)).start()

    for half, remote, sem in ((cube, 7, 0), (1 - cube, 8, 1)):
        arrived(q_land.at[0:remote], qz_r.at[sem])
        packed = q_land[pl.ds(half * 8, 8)].astype(F32)[:, 0:8, :].reshape(64, HD)
        q_row[7, half] = packed.astype(BF16)
        for p in range(7):
            send(q_row.at[7, half], q_row.at[p, half], qy_s, qy_r.at[p // 4], at_y(ORDER[p])).start()

    def pass_entries(g):
        first = g * 4 + (g * 4 == SELF)
        arrived(kv_all.at[0, first:g * 4 + 4], kz_r.at[g])
        part = slice(g * 4, g * 4 + 4)
        for s in (2, 1, 3):
            send(kv_all.at[0, part], kv_all.at[s, part], kx_s, kx_r.at[g], at_x(s)).start()

    for g in range(4):
        pass_entries(g)

    group = NX * 4 * TOK
    for g in range(4):
        part = slice(g * 4, g * 4 + 4)
        arrived(kv_all.at[1:4, part], kx_r.at[g])
        values = kv_all[:, part, TOK:2 * TOK, :].reshape(group, HD)
        vt[0:HD, g * group:(g + 1) * group] = values.astype(F32).T.astype(BF16)
    vt[HD:HD + 16, :] = jnp.ones((16, 4 * group), BF16)

    def own(p, g):
        return p == 7 and g == 2

    def rows_for(k):
        there = (1 - zl if k < 2 else zl) * 2 + cores[k % 2]
        return pl.ds(pl.multiple_of(there * 16, 16), 16)

    for near in (1, 0):
        arrived(q_row.at[near * 4:near * 4 + 4 - near], qy_r.at[near])
        for p in range(near * 4, near * 4 + 4):
            rows = q_row[p].astype(F32).reshape(2, 4, 2, 8, HD)
            for i in range(2):
                halves = [
                    jnp.where(mine == i, rows[c, k, 0], rows[c, k, 1]) for k in range(4) for c in range(2)
                ]
                q_all[i, p] = jnp.concatenate(halves, axis=0).astype(BF16)
    for unit in range(4):
        keys = jnp.concatenate(
            [kv_all[:, g * 4:g * 4 + 4, 0:TOK, :].reshape(group, HD) for g in range(4)], axis=0
        )
        queries = q_all[unit // 2, unit % 2 * 4:unit % 2 * 4 + 4].reshape(2 * HD, HD)
        scores = lax.dot_general(keys, queries, (((1,), (1,)), ((), ())), preferred_element_type=F32)
        top = jnp.max(scores, axis=0, keepdims=True) * SCALE2
        weights = jnp.exp2(scores * SCALE2 - top).astype(BF16)
        mixed = jnp.dot(vt[...], weights, preferred_element_type=F32)
        i, base = unit // 2, unit % 2 * 4
        total = mixed[HD:HD + 1, :]
        level = top + jnp.log2(total)
        rows = (mixed[0:HD, :] * (1.0 / total)).T.astype(BF16)
        for n in range(2):
            st_out[i, base // 2 + n] = level[:, n * HD:(n + 1) * HD]
        o_out[i, base:base + 4] = rows.reshape(4, 64, HD)
        for p in range(base, base + 4):
            for k in range(4):
                if not own(p, k):
                    dev = at_o(NY - ORDER[p], k < 2, k % 2)
                    send(st_out.at[i, p // 2], st_in.at[i, k, p], t_s.at[i, k], t_r.at[i, k], dev).start()
        for p in range(base, base + 4):
            for k in range(4):
                if not own(p, k):
                    dev = at_o(NY - ORDER[p], k < 2, k % 2)
                    piece = o_out.at[i, p, rows_for(k)]
                    send(piece, o_in.at[i, k, p], o_s.at[i, k], o_r.at[i, k], dev).start()

    row8 = lax.broadcasted_iota(jnp.int32, (8, HD), 0)
    lane8 = lax.broadcasted_iota(jnp.int32, (8, HD), 1)
    row = lax.broadcasted_iota(jnp.int32, (16, HD), 0)
    lane = lax.broadcasted_iota(jnp.int32, (16, HD), 1)
    straight = rem(lane, 16) == row
    valid = lax.broadcasted_iota(jnp.int32, (8, CW), 0) < count
    for i in range(2):
        st_in[i, 2, 7] = st_out[i, 3]
        o_in[i, 2, 7] = o_out[i, 7, rows_for(2)]
        levels = []
        for k in range(4):
            arrived(st_in.at[i, k, 0:8 - (k == 2)], t_r.at[i, k])
            seen = jnp.concatenate([st_in[i, k, p] for p in range(NY)], axis=0)
            seen = pltpu.roll(seen, 0, 1, stride=16, stride_axis=0)
            low = pltpu.roll(seen, rem(HD - quarter * 16, HD), 1)
            moved = jnp.where(rem(row8, 2) == 0, low, pltpu.roll(low, 64, 1))
            levels.append(jnp.sum(jnp.where(div(lane8, 16) == row8, moved, 0.0), axis=0, keepdims=True))
        levels = jnp.concatenate(levels + levels, axis=0)
        peak = levels
        for shift in (16, 32, 64):
            peak = jnp.maximum(peak, pltpu.roll(peak, shift, 1))
        parts = jnp.exp2(levels - peak)
        total = parts
        for shift in (16, 32, 64):
            total = total + pltpu.roll(total, shift, 1)
        shares = parts / total

        mean = []
        for k in range(4):
            arrived(o_in.at[i, k, 0:8 - (k == 2)], o_r.at[i, k])
            mix = jnp.where(straight, shares[k:k + 1, :], 0.0)
            mean.append(jnp.dot(mix.astype(BF16), o_in[i, k].reshape(HD, HD), preferred_element_type=F32))
        heads4 = [jnp.where(zl == z, mean[2 + dc], mean[dc]) for dc in range(2) for z in range(2)]
        rows = jnp.concatenate(heads4, axis=1).astype(BF16)

        if i == 0:
            loads[5].wait()
            send(w_hbm, w_all.at[1], w_s, w_r, at_z(0, 1)).wait_recv()
        for ci in range(CHUNKS):
            sides = []
            for start in (ci * CW, HALF + ci * CW):
                w = jnp.concatenate([w_all[0, :, start:start + CW], w_all[1, :, start:start + CW]], axis=0)
                sides.append(jnp.dot(rows, w, preferred_element_type=F32))
            for n in range(2):
                block = jnp.concatenate([side[n * 8:(n + 1) * 8] for side in sides], axis=0)
                p_out[i, n, ci] = block.astype(BF16)
            for slot, n in ((0, 1 - cube),) if i == 0 else ((1, cube), (2, 1 - cube)):
                dev = at_p(n, mine if i == 0 else 1 - mine)
                send(p_out.at[i, n, ci], p_in.at[slot, ci], p_s.at[slot], p_r.at[slot], dev).start()

    for slot in range(3):
        arrived(p_in.at[slot], p_r.at[slot])
    for ci in range(CHUNKS):
        total = p_out[0, cube, ci].astype(F32)
        for n in range(3):
            total = total + p_in[n, ci].astype(F32)
        out_ref[:, ci * CW:(ci + 1) * CW] = jnp.where(valid, total[0:8], 0.0)
        out_ref[:, HALF + ci * CW:HALF + (ci + 1) * CW] = jnp.where(valid, total[8:16], 0.0)

    left(q_out.at[0:15], qz_s)
    left(kv_out.at[0:15], kz_s)
    send(w_hbm, w_all.at[1], w_s, w_r, at_z(0, 1)).wait_send()
    left(q_row.at[0:7], qy_s)
    left(kv_all.at[1:4], kx_s)
    for i in range(2):
        for k in range(4):
            left(st_in.at[i, k, 0:8 - (k == 2)], t_s.at[i, k])
            left(o_in.at[i, k, 0:8 - (k == 2)], o_s.at[i, k])
    for slot in range(3):
        left(p_out.at[0, 0], p_s.at[slot])


def on_device(fresh_query, fresh_entries, cached_entries, recompute_rows, valid_counts, out_weight, out_gate):
    dma = pltpu.SemaphoreType.DMA
    width = HEADS * HD
    summed = pl.pallas_call(
        kernel,
        out_shape=pltpu.VMEM((8, D), F32),
        in_specs=[pl.BlockSpec(memory_space=pl.ANY)] * 6,
        out_specs=pl.BlockSpec(memory_space=pltpu.VMEM),
        scratch_shapes=[
            pltpu.VMEM((CAP, width), BF16),
            pltpu.VMEM((CAP, 2, width), BF16),
            pltpu.VMEM((2, TOK, width), BF16),
            pltpu.SMEM((1, CAP), jnp.int32),
            pltpu.SMEM((1, 1), jnp.int32),
            pltpu.VMEM((3, 8, width), F32),
            pltpu.VMEM((HEADS, 16, HD), BF16),
            pltpu.VMEM((HEADS, 2 * TOK, HD), BF16),
            pltpu.VMEM((HEADS, 16, HD), BF16),
            pltpu.VMEM((NX, HEADS, 2 * TOK, HD), BF16),
            pltpu.VMEM((NY, 2, 64, HD), BF16),
            pltpu.VMEM((2, NY, 64, HD), BF16),
            pltpu.VMEM((HD + 16, 4 * HEADS * TOK), BF16),
            pltpu.VMEM((2, NY, 64, HD), BF16),
            pltpu.VMEM((2, 4, NY, 16, HD), BF16),
            pltpu.VMEM((2, 4, 1, HD), F32),
            pltpu.VMEM((2, 4, NY, 1, HD), F32),
            pltpu.VMEM((2, 2 * HD, D), BF16),
            pltpu.VMEM((2, 2, CHUNKS, 16, CW), BF16),
            pltpu.VMEM((3, CHUNKS, 16, CW), BF16),
            dma((6,)),
            dma, dma((2,)), dma, dma((4,)),
            dma, dma,
            dma, dma((2,)),
            dma, dma((4,)),
            dma((2, 4)), dma((2, 4)), dma((2, 4)), dma((2, 4)),
            dma((3,)), dma((3,)),
        ],
        compiler_params=pltpu.CompilerParams(
            collective_id=0, has_side_effects=True, vmem_limit_bytes=60 * 1024 * 1024
        ),
    )(fresh_query, fresh_entries.transpose(1, 0, 2), cached_entries, recompute_rows, valid_counts.reshape(1, 1), out_weight)
    return (summed[:CAP] * out_gate[None, :]).astype(BF16)


def solution(mesh):
    both = ("head", "blk")
    in_specs = (P(both, None), P(None, both, None), P(None, both, None), P(both, None), P(both), P("head", None), P())
    return jax.shard_map(on_device, mesh=mesh, in_specs=in_specs, out_specs=P(both, None), check_vma=False)
```

```python
import functools
import math

import jax
import jax.numpy as jnp
from jax import lax
from jax.experimental import pallas as pl
from jax.experimental.pallas import tpu as pltpu
from jax.sharding import PartitionSpec as P

HD = 128
HEADS = 16
TOK = 16
CAP = 7
D = 3072
NX, NY, CHIPS = 4, 8, 8
CHUNKS = 3
HALF = D // 2
CW = HALF // CHUNKS
SCALE2 = (HD ** -0.5) * math.log2(math.e)
MESH = pl.DeviceIdType.MESH
F32, BF16 = jnp.float32, jnp.bfloat16

PLACES = [(dz, dc) for dz in range(CHIPS) for dc in range(2)]


def slots(groups):
    return {(dz, dc): g * 4 + dc * 2 + e for g, pair in enumerate(groups) for e, dz in enumerate(pair) for dc in range(2)}


SLOT = slots(((1, 7), (2, 6), (3, 5), (0, 4)))
SELF = SLOT[0, 0]
NEAR_FIRST = sorted((k for k in PLACES if k != (0, 0)), key=lambda k: min(k[0], CHIPS - k[0]))
FAR_FIRST = NEAR_FIRST[::-1]
ORDER = (4, 3, 5, 2, 6, 1, 7, 0)


def kernel(
    q_hbm, fresh_hbm, cached_hbm, rows_hbm, cnt_hbm, w_hbm, out_ref,
    q_in, fresh_in, cached_in, rows_in, cnt_in, fresh32, q_out, kv_out, q_land, kv_all, q_row, q_all, vt,
    o_out, o_in, st_out, st_in, w_all, p_out, p_in,
    sem_in, qz_s, qz_r, kz_s, kz_r, w_s, w_r, qy_s, qy_r, kx_s, kx_r, o_s, o_r, t_s, t_r, p_s, p_r,
):
    head = lax.axis_index("head")
    blk = lax.axis_index("blk")

    def div(a, b):
        return lax.div(a, jnp.int32(b))

    def rem(a, b):
        return lax.rem(a, jnp.int32(b))

    core, zh = rem(head, 2), div(head, 2)
    y, zl, x = rem(blk, NY), rem(div(blk, NY), 2), div(blk, 2 * NY)
    chip = zh * 2 + zl
    cube, mine = div(zh, 2), rem(zh, 2)
    quarter = zl * 2 + core
    place_here = cube * 8 + quarter * 2 + mine
    ups = [rem(chip + dz, CHIPS) for dz in range(CHIPS)]
    cores = [core, 1 - core]

    def at_z(dz, dc):
        return (div(ups[dz], 2) * 2 + cores[dc], (x * 2 + rem(ups[dz], 2)) * NY + y)

    def head_of(dz, dc):
        return div(ups[dz], 2) * 4 + cores[dc] * 2 + rem(ups[dz], 2)

    def at_x(dx):
        return (head, (rem(x + dx, NX) * 2 + zl) * NY + y)

    def at_y(dy):
        return (head, (x * 2 + zl) * NY + rem(y + dy, NY))

    def at_o(dy, odd, dc):
        return (zh * 2 + cores[dc], (x * 2 + (1 - zl if odd else zl)) * NY + rem(y + dy, NY))

    def at_p(half, n):
        return ((half * 2 + n) * 2 + core, blk)

    def send(src, dst, s_sem, r_sem, dev):
        return pltpu.make_async_remote_copy(
            src_ref=src, dst_ref=dst, send_sem=s_sem, recv_sem=r_sem,
            device_id=dev, device_id_type=MESH,
        )

    def arrived(ref, sem):
        send(ref, ref, sem, sem, at_x(1)).wait_recv()

    def left(ref, sem):
        send(ref, ref, sem, sem, at_x(1)).wait_send()

    loads = [
        pltpu.make_async_copy(q_hbm, q_in, sem_in.at[0]),
        pltpu.make_async_copy(fresh_hbm, fresh_in, sem_in.at[1]),
        pltpu.make_async_copy(cached_hbm, cached_in, sem_in.at[2]),
        pltpu.make_async_copy(rows_hbm, rows_in, sem_in.at[3]),
        pltpu.make_async_copy(cnt_hbm, cnt_in, sem_in.at[4]),
        pltpu.make_async_copy(w_hbm, w_all.at[0], sem_in.at[5]),
    ]
    loads[0].start()
    barrier = pltpu.get_barrier_semaphore()
    partners = [at_z(dz, dc) for dz, dc in FAR_FIRST]
    partners += [at_y(dy) for dy in ORDER[:7]] + [at_x(dx) for dx in (2, 1, 3)]
    for dev in partners[:15]:
        pl.semaphore_signal(barrier, inc=1, device_id=dev, device_id_type=MESH)
    for load in loads[1:5]:
        load.start()
    for dev in partners[15:]:
        pl.semaphore_signal(barrier, inc=1, device_id=dev, device_id_type=MESH)

    fresh32[0, ...] = jnp.zeros((8, HEADS * HD), F32)
    loads[0].wait()
    fresh32[0, 0:CAP, :] = q_in[...].astype(F32)

    def lanes(h):
        return pl.ds(pl.multiple_of(h * HD, HD), HD)

    for place in [(0, 0)] + FAR_FIRST:
        rows8 = fresh32[0, :, lanes(head_of(*place))]
        q_out[SLOT[place]] = jnp.concatenate([rows8, jnp.zeros((8, HD), F32)], axis=0).astype(BF16)
    q_land[place_here] = q_out[SELF]

    pl.semaphore_wait(barrier, len(partners))
    for place in FAR_FIRST:
        apart = rem(div(ups[place[0]], 4) + cube, 2)
        send(q_out.at[SLOT[place]], q_land.at[place_here], qz_s, qz_r.at[apart], at_z(*place)).start()

    for i in (1, 2, 3, 4):
        loads[i].wait()
    for i in range(2):
        fresh32[1 + i, 0:CAP, :] = fresh_in[:, i, :].astype(F32)
    count = cnt_in[0, 0]
    token = lax.broadcasted_iota(jnp.int32, (TOK, HD), 0)
    hits = []
    for c in range(CAP):
        used = jnp.full((TOK, HD), c, jnp.int32) < count
        hits.append((token == rows_in[0, c]) & used)

    def merged(h, i):
        rows = cached_in[i, :, lanes(h)].astype(F32)
        for c in range(CAP):
            rows = jnp.where(hits[c], fresh32[1 + i, c:c + 1, lanes(h)], rows)
        return rows.astype(BF16)

    for place in PLACES:
        for i in range(2):
            kv_out[SLOT[place], i * TOK:(i + 1) * TOK, :] = merged(head_of(*place), i)
    kv_all[0, SELF] = kv_out[SELF]

    for place in NEAR_FIRST:
        back = SLOT[(CHIPS - place[0]) % CHIPS, place[1]]
        send(kv_out.at[SLOT[place]], kv_all.at[0, back], kz_s, kz_r.at[back // 4], at_z(*place)).start()

    loads[5].start()
    send(w_hbm, w_all.at[1], w_s, w_r, at_z(0, 1)).start()

    for half, remote, sem in ((cube, 7, 0), (1 - cube, 8, 1)):
        arrived(q_land.at[0:remote], qz_r.at[sem])
        packed = q_land[pl.ds(half * 8, 8)].astype(F32)[:, 0:8, :].reshape(64, HD)
        q_row[7, half] = packed.astype(BF16)
        for p in range(7):
            send(q_row.at[7, half], q_row.at[p, half], qy_s, qy_r.at[p // 4], at_y(ORDER[p])).start()

    def pass_entries(g):
        first = g * 4 + (g * 4 == SELF)
        arrived(kv_all.at[0, first:g * 4 + 4], kz_r.at[g])
        part = slice(g * 4, g * 4 + 4)
        for s in (2, 1, 3):
            send(kv_all.at[0, part], kv_all.at[s, part], kx_s, kx_r.at[g], at_x(s)).start()

    for g in range(4):
        pass_entries(g)

    group = NX * 4 * TOK
    for g in range(4):
        part = slice(g * 4, g * 4 + 4)
        arrived(kv_all.at[1:4, part], kx_r.at[g])
        values = kv_all[:, part, TOK:2 * TOK, :].reshape(group, HD)
        vt[0:HD, g * group:(g + 1) * group] = values.astype(F32).T.astype(BF16)
    vt[HD:HD + 16, :] = jnp.ones((16, 4 * group), BF16)

    def own(p, g):
        return p == 7 and g == 2

    def rows_for(k):
        there = (1 - zl if k < 2 else zl) * 2 + cores[k % 2]
        return pl.ds(pl.multiple_of(there * 16, 16), 16)

    for near in (1, 0):
        arrived(q_row.at[near * 4:near * 4 + 4 - near], qy_r.at[near])
        for p in range(near * 4, near * 4 + 4):
            rows = q_row[p].astype(F32).reshape(2, 4, 2, 8, HD)
            for i in range(2):
                halves = [
                    jnp.where(mine == i, rows[c, k, 0], rows[c, k, 1]) for k in range(4) for c in range(2)
                ]
                q_all[i, p] = jnp.concatenate(halves, axis=0).astype(BF16)
    for unit in range(4):
        keys = jnp.concatenate(
            [kv_all[:, g * 4:g * 4 + 4, 0:TOK, :].reshape(group, HD) for g in range(4)], axis=0
        )
        queries = q_all[unit // 2, unit % 2 * 4:unit % 2 * 4 + 4].reshape(2 * HD, HD)
        scores = lax.dot_general(keys, queries, (((1,), (1,)), ((), ())), preferred_element_type=F32)
        top = jnp.max(scores, axis=0, keepdims=True) * SCALE2
        weights = jnp.exp2(scores * SCALE2 - top).astype(BF16)
        mixed = jnp.dot(vt[...], weights, preferred_element_type=F32)
        i, base = unit // 2, unit % 2 * 4
        total = mixed[HD:HD + 1, :]
        level = top + jnp.log2(total)
        rows = (mixed[0:HD, :] * (1.0 / total)).T.astype(BF16)
        for n in range(2):
            st_out[i, base // 2 + n] = level[:, n * HD:(n + 1) * HD]
        o_out[i, base:base + 4] = rows.reshape(4, 64, HD)
        for p in range(base, base + 4):
            for k in range(4):
                if not own(p, k):
                    dev = at_o(NY - ORDER[p], k < 2, k % 2)
                    send(st_out.at[i, p // 2], st_in.at[i, k, p], t_s.at[i, k], t_r.at[i, k], dev).start()
        for k in range(4):
            for p in range(base, base + 4):
                if not own(p, k):
                    dev = at_o(NY - ORDER[p], k < 2, k % 2)
                    piece = o_out.at[i, p, rows_for(k)]
                    send(piece, o_in.at[i, k, p], o_s.at[i, k], o_r.at[i, k], dev).start()

    row8 = lax.broadcasted_iota(jnp.int32, (8, HD), 0)
    lane8 = lax.broadcasted_iota(jnp.int32, (8, HD), 1)
    row = lax.broadcasted_iota(jnp.int32, (16, HD), 0)
    lane = lax.broadcasted_iota(jnp.int32, (16, HD), 1)
    straight = rem(lane, 16) == row
    valid = lax.broadcasted_iota(jnp.int32, (8, CW), 0) < count
    for i in range(2):
        st_in[i, 2, 7] = st_out[i, 3]
        o_in[i, 2, 7] = o_out[i, 7, rows_for(2)]
        levels = []
        for k in range(4):
            arrived(st_in.at[i, k, 0:8 - (k == 2)], t_r.at[i, k])
            seen = jnp.concatenate([st_in[i, k, p] for p in range(NY)], axis=0)
            seen = pltpu.roll(seen, 0, 1, stride=16, stride_axis=0)
            low = pltpu.roll(seen, rem(HD - quarter * 16, HD), 1)
            moved = jnp.where(rem(row8, 2) == 0, low, pltpu.roll(low, 64, 1))
            levels.append(jnp.sum(jnp.where(div(lane8, 16) == row8, moved, 0.0), axis=0, keepdims=True))
        levels = jnp.concatenate(levels + levels, axis=0)
        peak = levels
        for shift in (16, 32, 64):
            peak = jnp.maximum(peak, pltpu.roll(peak, shift, 1))
        parts = jnp.exp2(levels - peak)
        total = parts
        for shift in (16, 32, 64):
            total = total + pltpu.roll(total, shift, 1)
        shares = parts / total

        mean = []
        for k in range(4):
            arrived(o_in.at[i, k, 0:8 - (k == 2)], o_r.at[i, k])
            mix = jnp.where(straight, shares[k:k + 1, :], 0.0)
            mean.append(jnp.dot(mix.astype(BF16), o_in[i, k].reshape(HD, HD), preferred_element_type=F32))
        heads4 = [jnp.where(zl == z, mean[2 + dc], mean[dc]) for dc in range(2) for z in range(2)]
        rows = jnp.concatenate(heads4, axis=1).astype(BF16)

        if i == 0:
            loads[5].wait()
            send(w_hbm, w_all.at[1], w_s, w_r, at_z(0, 1)).wait_recv()
        for ci in range(CHUNKS):
            sides = []
            for start in (ci * CW, HALF + ci * CW):
                w = jnp.concatenate([w_all[0, :, start:start + CW], w_all[1, :, start:start + CW]], axis=0)
                sides.append(jnp.dot(rows, w, preferred_element_type=F32))
            for n in range(2):
                block = jnp.concatenate([side[n * 8:(n + 1) * 8] for side in sides], axis=0)
                p_out[i, n, ci] = block.astype(BF16)
            for slot, n in ((0, 1 - cube),) if i == 0 else ((1, cube), (2, 1 - cube)):
                dev = at_p(n, mine if i == 0 else 1 - mine)
                send(p_out.at[i, n, ci], p_in.at[slot, ci], p_s.at[slot], p_r.at[slot], dev).start()

    for slot in range(3):
        arrived(p_in.at[slot], p_r.at[slot])
    for ci in range(CHUNKS):
        total = p_out[0, cube, ci].astype(F32)
        for n in range(3):
            total = total + p_in[n, ci].astype(F32)
        out_ref[:, ci * CW:(ci + 1) * CW] = jnp.where(valid, total[0:8], 0.0)
        out_ref[:, HALF + ci * CW:HALF + (ci + 1) * CW] = jnp.where(valid, total[8:16], 0.0)

    left(q_out.at[0:15], qz_s)
    left(kv_out.at[0:15], kz_s)
    send(w_hbm, w_all.at[1], w_s, w_r, at_z(0, 1)).wait_send()
    left(q_row.at[0:7], qy_s)
    left(kv_all.at[1:4], kx_s)
    for i in range(2):
        for k in range(4):
            left(st_in.at[i, k, 0:8 - (k == 2)], t_s.at[i, k])
            left(o_in.at[i, k, 0:8 - (k == 2)], o_s.at[i, k])
    for slot in range(3):
        left(p_out.at[0, 0], p_s.at[slot])


def on_device(fresh_query, fresh_entries, cached_entries, recompute_rows, valid_counts, out_weight, out_gate):
    dma = pltpu.SemaphoreType.DMA
    width = HEADS * HD
    summed = pl.pallas_call(
        kernel,
        out_shape=pltpu.VMEM((8, D), F32),
        in_specs=[pl.BlockSpec(memory_space=pl.ANY)] * 6,
        out_specs=pl.BlockSpec(memory_space=pltpu.VMEM),
        scratch_shapes=[
            pltpu.VMEM((CAP, width), BF16),
            pltpu.VMEM((CAP, 2, width), BF16),
            pltpu.VMEM((2, TOK, width), BF16),
            pltpu.SMEM((1, CAP), jnp.int32),
            pltpu.SMEM((1, 1), jnp.int32),
            pltpu.VMEM((3, 8, width), F32),
            pltpu.VMEM((HEADS, 16, HD), BF16),
            pltpu.VMEM((HEADS, 2 * TOK, HD), BF16),
            pltpu.VMEM((HEADS, 16, HD), BF16),
            pltpu.VMEM((NX, HEADS, 2 * TOK, HD), BF16),
            pltpu.VMEM((NY, 2, 64, HD), BF16),
            pltpu.VMEM((2, NY, 64, HD), BF16),
            pltpu.VMEM((HD + 16, 4 * HEADS * TOK), BF16),
            pltpu.VMEM((2, NY, 64, HD), BF16),
            pltpu.VMEM((2, 4, NY, 16, HD), BF16),
            pltpu.VMEM((2, 4, 1, HD), F32),
            pltpu.VMEM((2, 4, NY, 1, HD), F32),
            pltpu.VMEM((2, 2 * HD, D), BF16),
            pltpu.VMEM((2, 2, CHUNKS, 16, CW), BF16),
            pltpu.VMEM((3, CHUNKS, 16, CW), BF16),
            dma((6,)),
            dma, dma((2,)), dma, dma((4,)),
            dma, dma,
            dma, dma((2,)),
            dma, dma((4,)),
            dma((2, 4)), dma((2, 4)), dma((2, 4)), dma((2, 4)),
            dma((3,)), dma((3,)),
        ],
        compiler_params=pltpu.CompilerParams(
            collective_id=0, has_side_effects=True, vmem_limit_bytes=60 * 1024 * 1024
        ),
    )(fresh_query, fresh_entries.transpose(1, 0, 2), cached_entries, recompute_rows, valid_counts.reshape(1, 1), out_weight)
    return (summed[:CAP] * out_gate[None, :]).astype(BF16)


def solution(mesh):
    both = ("head", "blk")
    in_specs = (P(both, None), P(None, both, None), P(None, both, None), P(both, None), P(both), P("head", None), P())
    return jax.shard_map(on_device, mesh=mesh, in_specs=in_specs, out_specs=P(both, None), check_vma=False)
```
